32 devices in a mesh: row: 2 (over y), col: 4 (over x, core), layer: 4 (over z).
Axes of the slice: x: 2, y: 2, z: 4, core: 2. Of those that a mesh axis runs over, the one named last changes fastest.
Arguments:
- panel: bfloat16 [2048, 4, 1024], P('row', 'layer', 'col'), may hold values from -6 to 6
- in_pattern: int32 [16, 4, 8], P('row', 'layer', 'col'), may hold values 0 or 1
- slab: bfloat16 [4, 8, 128, 2048], P('layer', 'row', None, 'col'), may hold values from -0.09375 to 0.09375
- owner: int32 [4, 8], P('layer'), may hold values from 0 to 7, each once within a row
- out_pattern: int32 [16, 16], P(('row', 'layer'), 'col'), may hold values 0 or 1
Outputs:
- product: bfloat16 [2048, 2048], P(('row', 'layer'), 'col')
The draws below stay inside these ranges and needn't reach their ends.
Inputs may be any that keep to these rules, and one draw needn't show every extreme that they name: `owner`: each row lists every number of 0 to 7 once.
All inputs are finite; a program needn't handle non-finite values. No bound on the sum of `in_pattern` or of `out_pattern` on one device may be relied on, other than what follows from the above.
Results may differ from the reference program's by a relative error of at most 0.001.
Values may be sent and summed in bfloat16 or wider, within the bound.
A program may use at most 64 MiB of HBM per device.

```python
import jax
import jax.numpy as jnp

BS = 128
MB = 16
KL = 8
NB = 16
N_LAYER = 4


def with_ends(drawn, stream_key, least, largest):
    index_at = [jax.random.randint(jax.random.fold_in(stream_key, axis), (), 0, length) for axis, length in enumerate(drawn.shape)]
    main_axis = drawn.shape.index(max(drawn.shape))
    neighbour = index_at[:main_axis] + [(index_at[main_axis] + 1) % drawn.shape[main_axis]] + index_at[main_axis + 1:]
    return drawn.at[tuple(index_at)].set(least).at[tuple(neighbour)].set(largest)


def levels(rng, shape, pieces, low, largest):
    loudness, own = 1.0, jax.random.fold_in(rng, 6)
    for dim, blocks in pieces:
        draws = jnp.exp(jax.random.uniform(jax.random.fold_in(own, dim), (blocks,), jnp.float32, low / len(pieces), largest / len(pieces)))
        loudness = loudness * jnp.repeat(draws, shape[dim] // blocks).reshape([-1 if axis == dim else 1 for axis in range(len(shape))])
    return loudness


def normal_values(rng, shape, scale, reach, cuts=(), kind=jnp.bfloat16):
    level = levels(rng, shape, cuts, -0.22, 0.18) if cuts else 1.0
    array = jax.random.normal(rng, shape, jnp.float32) * scale * level
    return jnp.minimum(jnp.maximum(array, -reach), reach).astype(kind)


def setup_inputs(seed: int = 0) -> dict:
    streams_of = jax.random.split(jax.random.key(seed), 6)
    return {
        "panel": normal_values(streams_of[0], (MB * BS, N_LAYER, KL * BS), 1.0, 6.0, ((0, 2), (1, 4), (2, 4))),
        "in_pattern": with_ends((jax.random.randint(streams_of[1], (MB, N_LAYER, KL), 0, 3) < 2).astype(jnp.int32), jax.random.fold_in(streams_of[1], 1), 0, 1),
        "slab": normal_values(streams_of[2], (N_LAYER, KL, BS, NB * BS), (N_LAYER * KL * BS) ** -0.5, 0.09375, ((0, 4), (1, 2), (3, 4))),
        "owner": jax.vmap(lambda own: jax.random.permutation(own, KL))(jax.random.split(streams_of[3], N_LAYER)).reshape((N_LAYER, KL)).astype(jnp.int32),
        "out_pattern": with_ends((jax.random.randint(streams_of[4], (MB, NB), 0, 4) < 3).astype(jnp.int32), jax.random.fold_in(streams_of[4], 1), 0, 1),
    }


def reference(panel, in_pattern, slab, owner, out_pattern):
    shaped = panel.reshape(MB, BS, N_LAYER, KL, BS)
    keeper = in_pattern.astype(jnp.bfloat16)[:, None, :, :, None]
    masked = (shaped * keeper).reshape(MB * BS, N_LAYER, KL * BS)
    running = jnp.zeros((MB * BS, NB * BS), jnp.float32)
    for layer_index in range(N_LAYER):
        picked = jnp.take(slab[layer_index], owner[layer_index].astype(jnp.int32), axis=0)
        picked = picked.reshape(KL * BS, NB * BS)
        running = running + jnp.dot(masked[:, layer_index, :], picked, preferred_element_type=jnp.float32)
    blocked = running.reshape(MB, BS, NB, BS) * out_pattern.astype(jnp.float32)[:, None, :, None]
    return blocked.reshape(MB * BS, NB * BS).astype(jnp.bfloat16)
```

```python
import functools

import jax
import jax.numpy as jnp
from jax import lax
from jax.experimental import pallas as pl
from jax.experimental.pallas import tpu as pltpu
from jax.sharding import PartitionSpec as P

MESH = pl.DeviceIdType.MESH
STEPS = 128.0
TOP = 32640.0
PAD = 16


def encode(values, out):
    rows = values.shape[0]
    peak = jnp.maximum(jnp.max(jnp.abs(values), axis=0, keepdims=True), 2.0**-100)
    level = jnp.ceil(jnp.log2(peak) * STEPS + 0.5)
    factor = jnp.exp2(level * (-1.0 / STEPS)) * TOP
    coded = jnp.round(values * factor).astype(jnp.int32)
    out[0:rows, :] = coded.astype(jnp.int16)
    wide = jnp.broadcast_to(level, (PAD, values.shape[1]))
    out[rows : rows + PAD, :] = wide.astype(jnp.int32).astype(jnp.int16)


def decode(message, rows):
    level = message[rows : rows + PAD, :].astype(jnp.int32).astype(jnp.float32)[0:1, :]
    factor = jnp.exp2(level * (1.0 / STEPS)) * (1.0 / TOP)
    return message[0:rows, :].astype(jnp.int32).astype(jnp.float32) * factor


def kernel(sizes, panel, in_pat, slab, owner, out_pat, out, *scratch):
    R, C, L, N = sizes
    slabs, ops = scratch[:N], scratch[N : 2 * N]
    portion, sbuf, rbuf, acc, sx, sc, sr, rp, ss, rs, sz, rz = scratch[2 * N :]
    H = C // 2
    row, col, z = lax.axis_index("row"), lax.axis_index("col"), lax.axis_index("layer")
    half, side = col // 2, col % 2
    mate = half * 2 + (1 - side)
    rows = out.shape[0]
    bs = slab.shape[2]
    depth = panel.shape[2]
    wide = out.shape[1] // N
    mine = slab.shape[1]
    brows = rows // bs
    hops = [((half + i) % H) * 2 + side for i in range(1, H)]
    relays = [((half + i) % H) * 2 + (1 - side) for i in range(1, H)]
    peers = [(row + i) % R for i in range(1, R)]

    barrier = pltpu.get_barrier_semaphore()
    for c in hops + [mate]:
        pl.semaphore_signal(barrier, inc=1, device_id={"col": c}, device_id_type=MESH)
    for r in peers:
        pl.semaphore_signal(barrier, inc=1, device_id={"row": r}, device_id_type=MESH)

    @pl.when(z > 0)
    def _():
        pl.semaphore_signal(barrier, inc=1, device_id={"layer": z - 1}, device_id_type=MESH)

    @pl.when(z < L - 1)
    def _():
        pl.semaphore_signal(barrier, inc=1, device_id={"layer": z + 1}, device_id_type=MESH)

    tables = [sorted(range(L), key=lambda d: (-abs(d - i), d)) for i in range(L)]

    def pick(t):
        found = 0
        for i in range(L):
            found = found + jnp.where(z == i, tables[i][t], 0)
        return found

    dest = [pick(t) for t in range(L)]

    def mask(t):
        for i in range(brows):
            first = pl.multiple_of(dest[t] * rows + i * bs, bs)
            for j in range(depth // bs):
                keep = in_pat[dest[t] * brows + i, 0, j].astype(jnp.float32)
                block = panel[pl.ds(first, bs), 0, j * bs : (j + 1) * bs].astype(jnp.float32)
                portion[col, t, i * bs : (i + 1) * bs, j * bs : (j + 1) * bs] = (block * keep).astype(jnp.bfloat16)

    def send_part(c_to, t, sem):
        return pltpu.make_async_remote_copy(
            src_ref=portion.at[col, t], dst_ref=portion.at[col, t], send_sem=sem, recv_sem=rp.at[col, t],
            device_id={"col": c_to}, device_id_type=MESH)

    def relay(c_from, t, sem):
        return pltpu.make_async_remote_copy(
            src_ref=portion.at[c_from, t], dst_ref=portion.at[c_from, t], send_sem=sem, recv_sem=rp.at[c_from, t],
            device_id={"col": mate}, device_id_type=MESH)

    def send_slab(r_to, i, n):
        return pltpu.make_async_remote_copy(
            src_ref=slab.at[0, :, :, pl.ds(n * wide, wide)], dst_ref=slabs[n].at[pl.ds(row * mine, mine)],
            send_sem=ss.at[i, n], recv_sem=rs.at[row, n], device_id={"row": r_to}, device_id_type=MESH)

    def start_parts(t):
        for i, c in enumerate(hops):
            send_part(c, t, sx.at[i, t]).start()
        send_part(mate, t, sc.at[t]).start()

    def start_slab(n):
        for i, r in enumerate(peers):
            send_slab(r, i, n).start()

    mask(0)
    pl.semaphore_wait(barrier, (R - 1) + H + jnp.where(z > 0, 1, 0) + jnp.where(z < L - 1, 1, 0))
    start_slab(0)
    start_parts(0)
    for t in range(1, L):
        mask(t)
        start_parts(t)
    for n in range(1, N):
        start_slab(n)
    for n in range(N):
        slabs[n][pl.ds(row * mine, mine)] = slab[0, :, :, n * wide : (n + 1) * wide]

    def ready_parts(t):
        for i, c in enumerate(hops):
            relay(c, t, sr.at[i, t]).wait_recv()
            relay(c, t, sr.at[i, t]).start()

    def wait_parts(t):
        for c in [mate] + relays:
            relay(c, t, sc.at[t]).wait_recv()

    def ready_slab(n):
        for r in peers:
            pltpu.make_async_remote_copy(
                src_ref=slabs[n].at[pl.ds(r * mine, mine)], dst_ref=slabs[n].at[pl.ds(r * mine, mine)],
                send_sem=ss.at[0, n], recv_sem=rs.at[r, n], device_id={"row": r}, device_id_type=MESH).wait_recv()
        for j in range(R * mine):
            ops[n][j * bs : (j + 1) * bs, :] = slabs[n][owner[0, j]]

    def product(t, n):
        total = jnp.dot(portion[0, t], ops[n][0:depth, :], preferred_element_type=jnp.float32)
        for c in range(1, C):
            total += jnp.dot(portion[c, t], ops[n][c * depth : (c + 1) * depth, :], preferred_element_type=jnp.float32)
        return total

    def message(t, n, slot, to):
        return pltpu.make_async_remote_copy(
            src_ref=sbuf.at[t, n], dst_ref=rbuf.at[slot, n], send_sem=sz.at[t, n], recv_sem=rz.at[slot, n],
            device_id={"layer": to}, device_id_type=MESH)

    def arrived(slot, n):
        message(0, n, slot, (z + 1) % L).wait_recv()
        return decode(rbuf.at[slot, n], rows)

    def route(t):
        up = jnp.where(dest[t] > z, 1, 0)
        return dest[t] + L * (1 - up), z + 2 * up - 1

    for n in range(N):
        for t in range(L - 1):
            if n == 0:
                ready_parts(t)
                if t == 0:
                    ready_slab(0)
                wait_parts(t)
            elif t == 0:
                ready_slab(n)
            slot, to = route(t)
            inner = (z > 0) & (z < L - 1)

            @pl.when(inner)
            def _(t=t, n=n, slot=slot):
                total = product(t, n)
                encode(total + arrived(slot, n), sbuf.at[t, n])

            @pl.when(jnp.logical_not(inner))
            def _(t=t, n=n):
                encode(product(t, n), sbuf.at[t, n])

            message(t, n, slot, to).start()

    ready_parts(L - 1)
    wait_parts(L - 1)
    for n in range(N):
        acc[:, n * wide : (n + 1) * wide] = product(L - 1, n)
    for n in range(N):
        here = slice(n * wide, (n + 1) * wide)

        @pl.when(z > 0)
        def _():
            acc[:, here] += arrived(z, n)

        @pl.when(z < L - 1)
        def _():
            acc[:, here] += arrived(z + L, n)

        for i in range(brows):
            for j in range(n * wide // bs, (n + 1) * wide // bs):
                keep = out_pat[i, j].astype(jnp.float32)
                at = (slice(i * bs, (i + 1) * bs), slice(j * bs, (j + 1) * bs))
                out[at] = (acc[at] * keep).astype(jnp.bfloat16)

    for t in range(L):
        for i, c in enumerate(hops):
            send_part(c, t, sx.at[i, t]).wait_send()
            relay(c, t, sr.at[i, t]).wait_send()
        send_part(mate, t, sc.at[t]).wait_send()
    for n in range(N):
        for i, r in enumerate(peers):
            send_slab(r, i, n).wait_send()
        for t in range(L - 1):
            slot, to = route(t)
            message(t, n, slot, to).wait_send()


def solution(mesh):
    R, C, L = (mesh.shape[name] for name in ("row", "col", "layer"))
    N = 2

    def shards(panel, in_pat, slab, owner, out_pat):
        bs, cols = slab.shape[2], slab.shape[3]
        rows = panel.shape[0] // L
        depth = panel.shape[2]
        blocks = R * slab.shape[1]
        wide = cols // N
        H = C // 2
        dma = pltpu.SemaphoreType.DMA
        vmem = pl.BlockSpec(memory_space=pltpu.VMEM)
        smem = pl.BlockSpec(memory_space=pltpu.SMEM)
        return pl.pallas_call(
            functools.partial(kernel, (R, C, L, N)),
            out_shape=jax.ShapeDtypeStruct((rows, cols), jnp.bfloat16),
            in_specs=[vmem, smem, vmem, smem, smem],
            out_specs=vmem,
            scratch_shapes=[pltpu.VMEM((blocks, bs, wide), jnp.bfloat16) for _ in range(N)]
            + [pltpu.VMEM((blocks * bs, wide), jnp.bfloat16) for _ in range(N)]
            + [
                pltpu.VMEM((C, L, rows, depth), jnp.bfloat16),
                pltpu.VMEM((L - 1, N, rows + PAD, wide), jnp.int16),
                pltpu.VMEM((2 * L, N, rows + PAD, wide), jnp.int16),
                pltpu.VMEM((rows, cols), jnp.float32),
                dma((H - 1, L)),
                dma((L,)),
                dma((H - 1, L)),
                dma((C, L)),
                dma((R - 1, N)),
                dma((R, N)),
                dma((L - 1, N)),
                dma((2 * L, N)),
            ],
            compiler_params=pltpu.CompilerParams(
                collective_id=0, has_side_effects=True, vmem_limit_bytes=48 * 2**20),
        )(panel, in_pat, slab, owner, out_pat)

    in_specs = (
        P("row", "layer", "col"),
        P("row", "layer", "col"),
        P("layer", "row", None, "col"),
        P("layer", None),
        P(("row", "layer"), "col"),
    )
    out_specs = P(("row", "layer"), "col")
    return jax.shard_map(shards, mesh=mesh, in_specs=in_specs, out_specs=out_specs, check_vma=False)
```

```python
import functools

import jax
import jax.numpy as jnp
from jax import lax
from jax.experimental import pallas as pl
from jax.experimental.pallas import tpu as pltpu
from jax.sharding import PartitionSpec as P

MESH = pl.DeviceIdType.MESH
STEPS = 128.0
TOP = 32640.0
PAD = 16


def encode(values, out):
    rows = values.shape[0]
    peak = jnp.maximum(jnp.max(jnp.abs(values), axis=0, keepdims=True), 2.0**-100)
    level = jnp.ceil(jnp.log2(peak) * STEPS + 0.5)
    factor = jnp.exp2(level * (-1.0 / STEPS)) * TOP
    coded = jnp.round(values * factor).astype(jnp.int32)
    out[0:rows, :] = coded.astype(jnp.int16)
    wide = jnp.broadcast_to(level, (PAD, values.shape[1]))
    out[rows : rows + PAD, :] = wide.astype(jnp.int32).astype(jnp.int16)


def decode(message, rows):
    level = message[rows : rows + PAD, :].astype(jnp.int32).astype(jnp.float32)[0:1, :]
    factor = jnp.exp2(level * (1.0 / STEPS)) * (1.0 / TOP)
    return message[0:rows, :].astype(jnp.int32).astype(jnp.float32) * factor


def kernel(sizes, panel, in_pat, slab, owner, out_pat, out, *scratch):
    R, C, L, N = sizes
    slabs, ops = scratch[:N], scratch[N : 2 * N]
    portion, sbuf, rbuf, acc, sx, sc, sr, rp, ss, rs, sz, rz = scratch[2 * N :]
    H = C // 2
    row, col, z = lax.axis_index("row"), lax.axis_index("col"), lax.axis_index("layer")
    half, side = col // 2, col % 2
    mate = half * 2 + (1 - side)
    rows = out.shape[0]
    bs = slab.shape[2]
    depth = panel.shape[1]
    wide = out.shape[1] // N
    mine = slab.shape[1]
    brows = rows // bs
    hops = [((half + i) % H) * 2 + side for i in range(1, H)]
    relays = [((half + i) % H) * 2 + (1 - side) for i in range(1, H)]
    peers = [(row + i) % R for i in range(1, R)]

    barrier = pltpu.get_barrier_semaphore()
    for c in hops + [mate]:
        pl.semaphore_signal(barrier, inc=1, device_id={"col": c}, device_id_type=MESH)
    for r in peers:
        pl.semaphore_signal(barrier, inc=1, device_id={"row": r}, device_id_type=MESH)

    @pl.when(z > 0)
    def _():
        pl.semaphore_signal(barrier, inc=1, device_id={"layer": z - 1}, device_id_type=MESH)

    @pl.when(z < L - 1)
    def _():
        pl.semaphore_signal(barrier, inc=1, device_id={"layer": z + 1}, device_id_type=MESH)

    tables = [sorted(range(L), key=lambda d: (-abs(d - i), d)) for i in range(L)]

    def pick(t):
        found = 0
        for i in range(L):
            found = found + jnp.where(z == i, tables[i][t], 0)
        return found

    dest = [pick(t) for t in range(L)]

    def mask(t):
        for i in range(brows):
            first = pl.multiple_of(dest[t] * rows + i * bs, bs)
            for j in range(depth // bs):
                keep = in_pat[j, dest[t] * brows + i].astype(jnp.float32)
                block = panel[pl.ds(first, bs), j * bs : (j + 1) * bs].astype(jnp.float32)
                portion[col, t, i * bs : (i + 1) * bs, j * bs : (j + 1) * bs] = (block * keep).astype(jnp.bfloat16)

    def send_part(c_to, t, sem):
        return pltpu.make_async_remote_copy(
            src_ref=portion.at[col, t], dst_ref=portion.at[col, t], send_sem=sem, recv_sem=rp.at[col, t],
            device_id={"col": c_to}, device_id_type=MESH)

    def relay(c_from, t, sem):
        return pltpu.make_async_remote_copy(
            src_ref=portion.at[c_from, t], dst_ref=portion.at[c_from, t], send_sem=sem, recv_sem=rp.at[c_from, t],
            device_id={"col": mate}, device_id_type=MESH)

    def send_slab(r_to, i, n):
        return pltpu.make_async_remote_copy(
            src_ref=slab.at[0, :, :, pl.ds(n * wide, wide)], dst_ref=slabs[n].at[pl.ds(row * mine, mine)],
            send_sem=ss.at[i, n], recv_sem=rs.at[row, n], device_id={"row": r_to}, device_id_type=MESH)

    def start_parts(t):
        for i, c in enumerate(hops):
            send_part(c, t, sx.at[i, t]).start()
        send_part(mate, t, sc.at[t]).start()

    def start_slab(n):
        for i, r in enumerate(peers):
            send_slab(r, i, n).start()

    mask(0)
    pl.semaphore_wait(barrier, (R - 1) + H + jnp.where(z > 0, 1, 0) + jnp.where(z < L - 1, 1, 0))
    for t in range(max(L, N)):
        if t < N:
            start_slab(t)
        if t < L:
            if t > 0:
                mask(t)
            start_parts(t)
    for n in range(N):
        slabs[n][pl.ds(row * mine, mine)] = slab[0, :, :, n * wide : (n + 1) * wide]

    def ready_parts(t):
        for i, c in enumerate(hops):
            relay(c, t, sr.at[i, t]).wait_recv()
            relay(c, t, sr.at[i, t]).start()

    def wait_parts(t):
        for c in [mate] + relays:
            relay(c, t, sc.at[t]).wait_recv()

    def ready_slab(n):
        for r in peers:
            pltpu.make_async_remote_copy(
                src_ref=slabs[n].at[pl.ds(r * mine, mine)], dst_ref=slabs[n].at[pl.ds(r * mine, mine)],
                send_sem=ss.at[0, n], recv_sem=rs.at[r, n], device_id={"row": r}, device_id_type=MESH).wait_recv()
        for j in range(R * mine):
            ops[n][j * bs : (j + 1) * bs, :] = slabs[n][owner[0, j]]

    def product(t, n):
        total = jnp.dot(portion[0, t], ops[n][0:depth, :], preferred_element_type=jnp.float32)
        for c in range(1, C):
            total += jnp.dot(portion[c, t], ops[n][c * depth : (c + 1) * depth, :], preferred_element_type=jnp.float32)
        return total

    def message(t, n, slot, to):
        return pltpu.make_async_remote_copy(
            src_ref=sbuf.at[t, n], dst_ref=rbuf.at[slot, n], send_sem=sz.at[t, n], recv_sem=rz.at[slot, n],
            device_id={"layer": to}, device_id_type=MESH)

    def arrived(slot, n):
        message(0, n, slot, (z + 1) % L).wait_recv()
        return decode(rbuf.at[slot, n], rows)

    def route(t):
        up = jnp.where(dest[t] > z, 1, 0)
        return dest[t] + L * (1 - up), z + 2 * up - 1

    for stage in range(max(L - 1, N)):
        if stage < L - 1:
            ready_parts(stage)
        if stage < N:
            ready_slab(stage)
        if stage < L - 1:
            wait_parts(stage)
        pieces = [(t, n) for t in range(L - 1) for n in range(N) if max(t, n) == stage]
        for t, n in sorted(pieces, key=lambda piece: (sum(piece), piece)):
            slot, to = route(t)
            inner = (z > 0) & (z < L - 1)

            @pl.when(inner)
            def _(t=t, n=n, slot=slot):
                total = product(t, n)
                encode(total + arrived(slot, n), sbuf.at[t, n])

            @pl.when(jnp.logical_not(inner))
            def _(t=t, n=n):
                encode(product(t, n), sbuf.at[t, n])

            message(t, n, slot, to).start()

    ready_parts(L - 1)
    wait_parts(L - 1)
    for n in range(N):
        acc[:, n * wide : (n + 1) * wide] = product(L - 1, n)
    for n in range(N):
        here = slice(n * wide, (n + 1) * wide)

        @pl.when(z > 0)
        def _():
            acc[:, here] += arrived(z, n)

        @pl.when(z < L - 1)
        def _():
            acc[:, here] += arrived(z + L, n)

        for i in range(brows):
            for j in range(n * wide // bs, (n + 1) * wide // bs):
                keep = out_pat[i, j].astype(jnp.float32)
                at = (slice(i * bs, (i + 1) * bs), slice(j * bs, (j + 1) * bs))
                out[at] = (acc[at] * keep).astype(jnp.bfloat16)

    for t in range(L):
        for i, c in enumerate(hops):
            send_part(c, t, sx.at[i, t]).wait_send()
            relay(c, t, sr.at[i, t]).wait_send()
        send_part(mate, t, sc.at[t]).wait_send()
    for n in range(N):
        for i, r in enumerate(peers):
            send_slab(r, i, n).wait_send()
        for t in range(L - 1):
            slot, to = route(t)
            message(t, n, slot, to).wait_send()


def solution(mesh):
    R, C, L = (mesh.shape[name] for name in ("row", "col", "layer"))
    N = 4

    def shards(panel, in_pat, slab, owner, out_pat):
        bs, cols = slab.shape[2], slab.shape[3]
        rows = panel.shape[0] // L
        depth = panel.shape[2]
        blocks = R * slab.shape[1]
        wide = cols // N
        H = C // 2
        dma = pltpu.SemaphoreType.DMA
        vmem = pl.BlockSpec(memory_space=pltpu.VMEM)
        smem = pl.BlockSpec(memory_space=pltpu.SMEM)
        return pl.pallas_call(
            functools.partial(kernel, (R, C, L, N)),
            out_shape=jax.ShapeDtypeStruct((rows, cols), jnp.bfloat16),
            in_specs=[vmem, smem, vmem, smem, smem],
            out_specs=vmem,
            scratch_shapes=[pltpu.VMEM((blocks, bs, wide), jnp.bfloat16) for _ in range(N)]
            + [pltpu.VMEM((blocks * bs, wide), jnp.bfloat16) for _ in range(N)]
            + [
                pltpu.VMEM((C, L, rows, depth), jnp.bfloat16),
                pltpu.VMEM((L - 1, N, rows + PAD, wide), jnp.int16),
                pltpu.VMEM((2 * L, N, rows + PAD, wide), jnp.int16),
                pltpu.VMEM((rows, cols), jnp.float32),
                dma((H - 1, L)),
                dma((L,)),
                dma((H - 1, L)),
                dma((C, L)),
                dma((R - 1, N)),
                dma((R, N)),
                dma((L - 1, N)),
                dma((2 * L, N)),
            ],
            compiler_params=pltpu.CompilerParams(
                collective_id=0, has_side_effects=True, vmem_limit_bytes=48 * 2**20),
        )(panel.reshape(panel.shape[0], depth), in_pat[:, 0, :].T, slab, owner, out_pat)

    in_specs = (
        P("row", "layer", "col"),
        P("row", "layer", "col"),
        P("layer", "row", None, "col"),
        P("layer", None),
        P(("row", "layer"), "col"),
    )
    out_specs = P(("row", "layer"), "col")
    return jax.shard_map(shards, mesh=mesh, in_specs=in_specs, out_specs=out_specs, check_vma=False)
```

```python
import functools

import jax
import jax.numpy as jnp
from jax import lax
from jax.experimental import pallas as pl
from jax.experimental.pallas import tpu as pltpu
from jax.sharding import PartitionSpec as P

MESH = pl.DeviceIdType.MESH
STEPS = 128.0
TOP = 32640.0
PAD = 16


def encode(values, out):
    rows = values.shape[0]
    peak = jnp.maximum(jnp.max(jnp.abs(values), axis=0, keepdims=True), 2.0**-100)
    level = jnp.ceil(jnp.log2(peak) * STEPS + 0.5)
    factor = jnp.exp2(level * (-1.0 / STEPS)) * TOP
    coded = jnp.round(values * factor).astype(jnp.int32)
    out[0:rows, :] = coded.astype(jnp.int16)
    wide = jnp.broadcast_to(level, (PAD, values.shape[1]))
    out[rows : rows + PAD, :] = wide.astype(jnp.int32).astype(jnp.int16)


def decode(message, rows):
    level = message[rows : rows + PAD, :].astype(jnp.int32).astype(jnp.float32)[0:1, :]
    factor = jnp.exp2(level * (1.0 / STEPS)) * (1.0 / TOP)
    return message[0:rows, :].astype(jnp.int32).astype(jnp.float32) * factor


def kernel(sizes, widths, panel_hbm, in_hbm, slab_hbm, owner_hbm, out_hbm, out, *scratch):
    R, C, L = sizes
    N = len(widths)
    starts = [sum(widths[:n]) for n in range(N)]
    slabs, ops, sbufs, rbufs = (scratch[i * N : (i + 1) * N] for i in range(4))
    panel, in_pat, owner, out_pat, portion, acc, lp, ls, lm, sx, sc, sr, rp, ss, rs, sz, rz = scratch[4 * N :]
    H = C // 2
    row, col, z = lax.axis_index("row"), lax.axis_index("col"), lax.axis_index("layer")
    half, side = col // 2, col % 2
    mate = half * 2 + (1 - side)
    rows = out.shape[0]
    bs = slab_hbm.shape[2]
    depth = panel.shape[1]
    mine = slab_hbm.shape[1]
    brows = rows // bs
    hops = [((half + i) % H) * 2 + side for i in range(1, H)]
    relays = [((half + i) % H) * 2 + (1 - side) for i in range(1, H)]
    peers = [(row + i) % R for i in range(1, R)]

    barrier = pltpu.get_barrier_semaphore()
    for c in hops + [mate]:
        pl.semaphore_signal(barrier, inc=1, device_id={"col": c}, device_id_type=MESH)
    for r in peers:
        pl.semaphore_signal(barrier, inc=1, device_id={"row": r}, device_id_type=MESH)

    @pl.when(z > 0)
    def _():
        pl.semaphore_signal(barrier, inc=1, device_id={"layer": z - 1}, device_id_type=MESH)

    @pl.when(z < L - 1)
    def _():
        pl.semaphore_signal(barrier, inc=1, device_id={"layer": z + 1}, device_id_type=MESH)

    tables = [sorted(range(L), key=lambda d: (-abs(d - i), d)) for i in range(L)]

    def pick(t):
        found = 0
        for i in range(L):
            found = found + jnp.where(z == i, tables[i][t], 0)
        return found

    dest = [pick(t) for t in range(L)]

    def load_panel(t):
        here = pl.ds(pl.multiple_of(dest[t] * rows, rows), rows)
        return pltpu.make_async_copy(panel_hbm.at[here], panel.at[here], lp.at[t])

    def load_slab(n):
        return pltpu.make_async_copy(
            slab_hbm.at[0, :, :, pl.ds(starts[n], widths[n])], slabs[n].at[pl.ds(row * mine, mine)], ls.at[n])

    small = [
        pltpu.make_async_copy(src, dst, lm.at[i])
        for i, (src, dst) in enumerate([(in_hbm, in_pat), (owner_hbm, owner), (out_hbm, out_pat)])
    ]
    small[0].start()
    load_panel(0).start()
    load_slab(0).start()
    for t in range(1, max(L, N)):
        if t < L:
            load_panel(t).start()
        if t < N:
            load_slab(t).start()
    small[1].start()
    small[2].start()

    def mask(t):
        for i in range(brows):
            first = pl.multiple_of(dest[t] * rows + i * bs, bs)
            for j in range(depth // bs):
                keep = in_pat[j, dest[t] * brows + i].astype(jnp.float32)
                block = panel[pl.ds(first, bs), j * bs : (j + 1) * bs].astype(jnp.float32)
                portion[col, t, i * bs : (i + 1) * bs, j * bs : (j + 1) * bs] = (block * keep).astype(jnp.bfloat16)

    def send_part(c_to, t, sem):
        return pltpu.make_async_remote_copy(
            src_ref=portion.at[col, t], dst_ref=portion.at[col, t], send_sem=sem, recv_sem=rp.at[col, t],
            device_id={"col": c_to}, device_id_type=MESH)

    def relay(c_from, t, sem):
        return pltpu.make_async_remote_copy(
            src_ref=portion.at[c_from, t], dst_ref=portion.at[c_from, t], send_sem=sem, recv_sem=rp.at[c_from, t],
            device_id={"col": mate}, device_id_type=MESH)

    def send_slab(r_to, i, n):
        block = slabs[n].at[pl.ds(row * mine, mine)]
        return pltpu.make_async_remote_copy(
            src_ref=block, dst_ref=block, send_sem=ss.at[i, n], recv_sem=rs.at[row, n],
            device_id={"row": r_to}, device_id_type=MESH)

    def start_parts(t):
        for i, c in enumerate(hops):
            send_part(c, t, sx.at[i, t]).start()
        send_part(mate, t, sc.at[t]).start()

    def start_slab(n):
        for i, r in enumerate(peers):
            send_slab(r, i, n).start()

    small[0].wait()
    load_panel(0).wait()
    mask(0)
    load_slab(0).wait()
    pl.semaphore_wait(barrier, (R - 1) + H + jnp.where(z > 0, 1, 0) + jnp.where(z < L - 1, 1, 0))
    start_slab(0)
    start_parts(0)
    for t in range(1, max(L, N)):
        if t < N:
            load_slab(t).wait()
            start_slab(t)
        if t < L:
            load_panel(t).wait()
            mask(t)
            start_parts(t)
    small[1].wait()
    small[2].wait()

    def ready_parts(t):
        for i, c in enumerate(hops):
            relay(c, t, sr.at[i, t]).wait_recv()
            relay(c, t, sr.at[i, t]).start()

    def wait_parts(t):
        for c in [mate] + relays:
            relay(c, t, sc.at[t]).wait_recv()

    def ready_slab(n):
        for r in peers:
            pltpu.make_async_remote_copy(
                src_ref=slabs[n].at[pl.ds(r * mine, mine)], dst_ref=slabs[n].at[pl.ds(r * mine, mine)],
                send_sem=ss.at[0, n], recv_sem=rs.at[r, n], device_id={"row": r}, device_id_type=MESH).wait_recv()
        for j in range(R * mine):
            ops[n][j * bs : (j + 1) * bs, :] = slabs[n][owner[0, j]]

    def product(t, n):
        total = jnp.dot(portion[0, t], ops[n][0:depth, :], preferred_element_type=jnp.float32)
        for c in range(1, C):
            total += jnp.dot(portion[c, t], ops[n][c * depth : (c + 1) * depth, :], preferred_element_type=jnp.float32)
        return total

    def message(t, n, slot, to):
        return pltpu.make_async_remote_copy(
            src_ref=sbufs[n].at[t], dst_ref=rbufs[n].at[slot], send_sem=sz.at[t, n], recv_sem=rz.at[slot, n],
            device_id={"layer": to}, device_id_type=MESH)

    def arrived(slot, n):
        message(0, n, slot, (z + 1) % L).wait_recv()
        return decode(rbufs[n].at[slot], rows)

    def route(t):
        up = jnp.where(dest[t] > z, 1, 0)
        return dest[t] + L * (1 - up), z + 2 * up - 1

    inner = (z > 0) & (z < L - 1)

    def pass_on(t, n):
        slot, to = route(t)

        @pl.when(inner)
        def _():
            total = product(t, n)
            encode(total + arrived(slot, n), sbufs[n].at[t])

        @pl.when(jnp.logical_not(inner))
        def _():
            encode(product(t, n), sbufs[n].at[t])

        message(t, n, slot, to).start()

    for stage in range(max(L - 1, N)):
        last = stage == max(L - 1, N) - 1
        if stage < L - 1:
            ready_parts(stage)
            if stage == 0:
                ready_slab(0)
            wait_parts(stage)
            for n in range(min(stage, N)):
                pass_on(stage, n)
        if 0 < stage < N:
            ready_slab(stage)
        if stage < N:
            for t in range(min(stage + 1, L - 1)):
                pass_on(t, stage)
                if last and t == 0:
                    ready_parts(L - 1)
                    wait_parts(L - 1)
                    for n in range(N):
                        acc[:, starts[n] : starts[n] + widths[n]] = product(L - 1, n)

    for n in range(N):
        here = slice(starts[n], starts[n] + widths[n])

        @pl.when(z > 0)
        def _():
            acc[:, here] += arrived(z, n)

        @pl.when(z < L - 1)
        def _():
            acc[:, here] += arrived(z + L, n)

        for i in range(brows):
            for j in range(starts[n] // bs, (starts[n] + widths[n]) // bs):
                keep = out_pat[i, j].astype(jnp.float32)
                at = (slice(i * bs, (i + 1) * bs), slice(j * bs, (j + 1) * bs))
                out[at] = (acc[at] * keep).astype(jnp.bfloat16)

    for t in range(L):
        for i, c in enumerate(hops):
            send_part(c, t, sx.at[i, t]).wait_send()
            relay(c, t, sr.at[i, t]).wait_send()
        send_part(mate, t, sc.at[t]).wait_send()
    for n in range(N):
        for i, r in enumerate(peers):
            send_slab(r, i, n).wait_send()
        for t in range(L - 1):
            slot, to = route(t)
            message(t, n, slot, to).wait_send()


def solution(mesh):
    R, C, L = (mesh.shape[name] for name in ("row", "col", "layer"))

    def shards(panel, in_pat, slab, owner, out_pat):
        bs, cols = slab.shape[2], slab.shape[3]
        rows = panel.shape[0] // L
        depth = panel.shape[2]
        blocks = R * slab.shape[1]
        widths = (cols // 4, cols // 4, cols // 2)
        N = len(widths)
        H = C // 2
        dma = pltpu.SemaphoreType.DMA
        vmem = pl.BlockSpec(memory_space=pltpu.VMEM)
        hbm = pl.BlockSpec(memory_space=pl.ANY)
        return pl.pallas_call(
            functools.partial(kernel, (R, C, L), widths),
            out_shape=jax.ShapeDtypeStruct((rows, cols), jnp.bfloat16),
            in_specs=[hbm] * 5,
            out_specs=vmem,
            scratch_shapes=[pltpu.VMEM((blocks, bs, w), jnp.bfloat16) for w in widths]
            + [pltpu.VMEM((blocks * bs, w), jnp.bfloat16) for w in widths]
            + [pltpu.VMEM((L - 1, rows + PAD, w), jnp.int16) for w in widths]
            + [pltpu.VMEM((2 * L, rows + PAD, w), jnp.int16) for w in widths]
            + [
                pltpu.VMEM((panel.shape[0], depth), jnp.bfloat16),
                pltpu.SMEM((in_pat.shape[2], in_pat.shape[0]), jnp.int32),
                pltpu.SMEM(owner.shape, jnp.int32),
                pltpu.SMEM(out_pat.shape, jnp.int32),
                pltpu.VMEM((C, L, rows, depth), jnp.bfloat16),
                pltpu.VMEM((rows, cols), jnp.float32),
                dma((L,)),
                dma((N,)),
                dma((3,)),
                dma((H - 1, L)),
                dma((L,)),
                dma((H - 1, L)),
                dma((C, L)),
                dma((R - 1, N)),
                dma((R, N)),
                dma((L - 1, N)),
                dma((2 * L, N)),
            ],
            compiler_params=pltpu.CompilerParams(
                collective_id=0, has_side_effects=True, vmem_limit_bytes=56 * 2**20),
        )(panel.reshape(panel.shape[0], depth), in_pat[:, 0, :].T, slab, owner, out_pat)

    in_specs = (
        P("row", "layer", "col"),
        P("row", "layer", "col"),
        P("layer", "row", None, "col"),
        P("layer", None),
        P(("row", "layer"), "col"),
    )
    out_specs = P(("row", "layer"), "col")
    return jax.shard_map(shards, mesh=mesh, in_specs=in_specs, out_specs=out_specs, check_vma=False)
```

```python
import functools

import jax
import jax.numpy as jnp
from jax import lax
from jax.experimental import pallas as pl
from jax.experimental.pallas import tpu as pltpu
from jax.sharding import PartitionSpec as P

MESH = pl.DeviceIdType.MESH
STEPS = 128.0
TOP = 32640.0
PAD = 16


def encode(values, out):
    rows = values.shape[0]
    peak = jnp.maximum(jnp.max(jnp.abs(values), axis=0, keepdims=True), 2.0**-100)
    level = jnp.ceil(jnp.log2(peak) * STEPS + 0.5)
    factor = jnp.exp2(level * (-1.0 / STEPS)) * TOP
    coded = jnp.round(values * factor).astype(jnp.int32)
    out[0:rows, :] = coded.astype(jnp.int16)
    wide = jnp.broadcast_to(level, (PAD, values.shape[1]))
    out[rows : rows + PAD, :] = wide.astype(jnp.int32).astype(jnp.int16)


def decode(message, rows):
    level = message[rows : rows + PAD, :].astype(jnp.int32).astype(jnp.float32)[0:1, :]
    factor = jnp.exp2(level * (1.0 / STEPS)) * (1.0 / TOP)
    return message[0:rows, :].astype(jnp.int32).astype(jnp.float32) * factor


def kernel(sizes, widths, panel_hbm, in_hbm, slab_hbm, owner_hbm, out_hbm, out, *scratch):
    R, C, L = sizes
    N = len(widths)
    starts = [sum(widths[:n]) for n in range(N)]
    slabs, ops, sbufs, rbufs = (scratch[i * N : (i + 1) * N] for i in range(4))
    panel, in_pat, owner, out_pat, portion, acc, lp, ls, lm, sx, sc, sr, rp, ss, rs, sz, rz = scratch[4 * N :]
    H = C // 2
    row, col, z = lax.axis_index("row"), lax.axis_index("col"), lax.axis_index("layer")
    half, side = col // 2, col % 2
    mate = half * 2 + (1 - side)
    rows = out.shape[0]
    bs = slab_hbm.shape[2]
    depth = panel.shape[1]
    mine = slab_hbm.shape[1]
    brows = rows // bs
    hops = [((half + i) % H) * 2 + side for i in range(1, H)]
    relays = [((half + i) % H) * 2 + (1 - side) for i in range(1, H)]
    peers = [(row + i) % R for i in range(1, R)]

    barrier = pltpu.get_barrier_semaphore()
    for c in hops + [mate]:
        pl.semaphore_signal(barrier, inc=1, device_id={"col": c}, device_id_type=MESH)
    for r in peers:
        pl.semaphore_signal(barrier, inc=1, device_id={"row": r}, device_id_type=MESH)

    @pl.when(z > 0)
    def _():
        pl.semaphore_signal(barrier, inc=1, device_id={"layer": z - 1}, device_id_type=MESH)

    @pl.when(z < L - 1)
    def _():
        pl.semaphore_signal(barrier, inc=1, device_id={"layer": z + 1}, device_id_type=MESH)

    tables = [sorted(range(L), key=lambda d: (-abs(d - i), -i if d > i else i - L + 1)) for i in range(L)]

    def pick(t):
        found = 0
        for i in range(L):
            found = found + jnp.where(z == i, tables[i][t], 0)
        return found

    dest = [pick(t) for t in range(L)]

    def load_panel(t):
        here = pl.ds(pl.multiple_of(dest[t] * rows, rows), rows)
        return pltpu.make_async_copy(panel_hbm.at[here], panel.at[here], lp.at[t])

    def load_slab(n):
        return pltpu.make_async_copy(
            slab_hbm.at[0, :, :, pl.ds(starts[n], widths[n])], slabs[n].at[pl.ds(row * mine, mine)], ls.at[n])

    small = [
        pltpu.make_async_copy(src, dst, lm.at[i])
        for i, (src, dst) in enumerate([(in_hbm, in_pat), (owner_hbm, owner), (out_hbm, out_pat)])
    ]
    small[0].start()
    load_panel(0).start()
    load_slab(0).start()
    for t in range(1, max(L, N)):
        if t < L:
            load_panel(t).start()
        if t < N:
            load_slab(t).start()
    small[1].start()
    small[2].start()

    def mask(t):
        for i in range(brows):
            first = pl.multiple_of(dest[t] * rows + i * bs, bs)
            for j in range(depth // bs):
                keep = in_pat[j, dest[t] * brows + i].astype(jnp.float32)
                block = panel[pl.ds(first, bs), j * bs : (j + 1) * bs].astype(jnp.float32)
                portion[col, t, i * bs : (i + 1) * bs, j * bs : (j + 1) * bs] = (block * keep).astype(jnp.bfloat16)

    def send_part(c_to, t, sem):
        return pltpu.make_async_remote_copy(
            src_ref=portion.at[col, t], dst_ref=portion.at[col, t], send_sem=sem, recv_sem=rp.at[col, t],
            device_id={"col": c_to}, device_id_type=MESH)

    def relay(c_from, t, sem):
        return pltpu.make_async_remote_copy(
            src_ref=portion.at[c_from, t], dst_ref=portion.at[c_from, t], send_sem=sem, recv_sem=rp.at[c_from, t],
            device_id={"col": mate}, device_id_type=MESH)

    def send_slab(r_to, i, n):
        block = slabs[n].at[pl.ds(row * mine, mine)]
        return pltpu.make_async_remote_copy(
            src_ref=block, dst_ref=block, send_sem=ss.at[i, n], recv_sem=rs.at[row, n],
            device_id={"row": r_to}, device_id_type=MESH)

    def start_parts(t):
        for i, c in enumerate(hops):
            send_part(c, t, sx.at[i, t]).start()
        send_part(mate, t, sc.at[t]).start()

    def start_slab(n):
        for i, r in enumerate(peers):
            send_slab(r, i, n).start()

    small[0].wait()
    load_panel(0).wait()
    mask(0)
    load_slab(0).wait()
    pl.semaphore_wait(barrier, (R - 1) + H + jnp.where(z > 0, 1, 0) + jnp.where(z < L - 1, 1, 0))
    start_slab(0)
    start_parts(0)
    for t in range(1, max(L, N)):
        if t < N:
            load_slab(t).wait()
            start_slab(t)
        if t < L:
            load_panel(t).wait()
            mask(t)
            start_parts(t)
    small[1].wait()
    small[2].wait()

    def ready_parts(t):
        for i, c in enumerate(hops):
            relay(c, t, sr.at[i, t]).wait_recv()
            relay(c, t, sr.at[i, t]).start()

    def wait_parts(t):
        for c in [mate] + relays:
            relay(c, t, sc.at[t]).wait_recv()

    def ready_slab(n):
        for r in peers:
            pltpu.make_async_remote_copy(
                src_ref=slabs[n].at[pl.ds(r * mine, mine)], dst_ref=slabs[n].at[pl.ds(r * mine, mine)],
                send_sem=ss.at[0, n], recv_sem=rs.at[r, n], device_id={"row": r}, device_id_type=MESH).wait_recv()
        for j in range(R * mine):
            ops[n][j * bs : (j + 1) * bs, :] = slabs[n][owner[0, j]]

    def product(t, n):
        left = jnp.concatenate([portion[c, t] for c in range(C)], axis=1)
        return jnp.dot(left, ops[n][...], preferred_element_type=jnp.float32)

    def message(t, n, slot, to):
        return pltpu.make_async_remote_copy(
            src_ref=sbufs[n].at[t], dst_ref=rbufs[n].at[slot], send_sem=sz.at[t, n], recv_sem=rz.at[slot, n],
            device_id={"layer": to}, device_id_type=MESH)

    def arrived(slot, n):
        message(0, n, slot, (z + 1) % L).wait_recv()
        return decode(rbufs[n].at[slot], rows)

    def route(t):
        up = jnp.where(dest[t] > z, 1, 0)
        return dest[t] + L * (1 - up), z + 2 * up - 1

    inner = (z > 0) & (z < L - 1)

    def pass_on(t, n):
        slot, to = route(t)

        @pl.when(inner)
        def _():
            total = product(t, n)
            encode(total + arrived(slot, n), sbufs[n].at[t])

        @pl.when(jnp.logical_not(inner))
        def _():
            encode(product(t, n), sbufs[n].at[t])

        message(t, n, slot, to).start()

    ready_parts(0)
    ready_slab(0)
    wait_parts(0)
    pass_on(0, 0)
    for n in range(1, N):
        ready_slab(n)
        pass_on(0, n)
        if n == 1 and L > 2:
            ready_parts(1)
            wait_parts(1)
            pass_on(1, 0)
        if n == N - 1:
            for t in range(min(2, L - 1), L):
                ready_parts(t)
            for t in range(min(2, L - 1), L):
                wait_parts(t)
            for m in range(N):
                acc[:, starts[m] : starts[m] + widths[m]] = product(L - 1, m)
        if L > 2:
            pass_on(1, n)
    for t in range(2, L - 1):
        for n in range(N):
            pass_on(t, n)

    for n in range(N):
        here = slice(starts[n], starts[n] + widths[n])

        @pl.when(z > 0)
        def _():
            acc[:, here] += arrived(z, n)

        @pl.when(z < L - 1)
        def _():
            acc[:, here] += arrived(z + L, n)

        for i in range(brows):
            for j in range(starts[n] // bs, (starts[n] + widths[n]) // bs):
                keep = out_pat[i, j].astype(jnp.float32)
                at = (slice(i * bs, (i + 1) * bs), slice(j * bs, (j + 1) * bs))
                out[at] = (acc[at] * keep).astype(jnp.bfloat16)

    for t in range(L):
        for i, c in enumerate(hops):
            send_part(c, t, sx.at[i, t]).wait_send()
            relay(c, t, sr.at[i, t]).wait_send()
        send_part(mate, t, sc.at[t]).wait_send()
    for n in range(N):
        for i, r in enumerate(peers):
            send_slab(r, i, n).wait_send()
        for t in range(L - 1):
            slot, to = route(t)
            message(t, n, slot, to).wait_send()


def solution(mesh):
    R, C, L = (mesh.shape[name] for name in ("row", "col", "layer"))

    def shards(panel, in_pat, slab, owner, out_pat):
        bs, cols = slab.shape[2], slab.shape[3]
        rows = panel.shape[0] // L
        depth = panel.shape[2]
        blocks = R * slab.shape[1]
        widths = (cols // 4,) * 4
        N = len(widths)
        H = C // 2
        dma = pltpu.SemaphoreType.DMA
        vmem = pl.BlockSpec(memory_space=pltpu.VMEM)
        hbm = pl.BlockSpec(memory_space=pltpu.HBM)
        return pl.pallas_call(
            functools.partial(kernel, (R, C, L), widths),
            out_shape=jax.ShapeDtypeStruct((rows, cols), jnp.bfloat16),
            in_specs=[hbm] * 5,
            out_specs=vmem,
            scratch_shapes=[pltpu.VMEM((blocks, bs, w), jnp.bfloat16) for w in widths]
            + [pltpu.VMEM((blocks * bs, w), jnp.bfloat16) for w in widths]
            + [pltpu.VMEM((L - 1, rows + PAD, w), jnp.int16) for w in widths]
            + [pltpu.VMEM((2 * L, rows + PAD, w), jnp.int16) for w in widths]
            + [
                pltpu.VMEM((panel.shape[0], depth), jnp.bfloat16),
                pltpu.SMEM((in_pat.shape[2], in_pat.shape[0]), jnp.int32),
                pltpu.SMEM(owner.shape, jnp.int32),
                pltpu.SMEM(out_pat.shape, jnp.int32),
                pltpu.VMEM((C, L, rows, depth), jnp.bfloat16),
                pltpu.VMEM((rows, cols), jnp.float32),
                dma((L,)),
                dma((N,)),
                dma((3,)),
                dma((H - 1, L)),
                dma((L,)),
                dma((H - 1, L)),
                dma((C, L)),
                dma((R - 1, N)),
                dma((R, N)),
                dma((L - 1, N)),
                dma((2 * L, N)),
            ],
            compiler_params=pltpu.CompilerParams(
                collective_id=0, has_side_effects=True, vmem_limit_bytes=56 * 2**20),
        )(panel.reshape(panel.shape[0], depth), in_pat[:, 0, :].T, slab, owner, out_pat)

    in_specs = (
        P("row", "layer", "col"),
        P("row", "layer", "col"),
        P("layer", "row", None, "col"),
        P("layer", None),
        P(("row", "layer"), "col"),
    )
    out_specs = P(("row", "layer"), "col")
    return jax.shard_map(shards, mesh=mesh, in_specs=in_specs, out_specs=out_specs, check_vma=False)
```

```python
import functools

import jax
import jax.numpy as jnp
from jax import lax
from jax.experimental import pallas as pl
from jax.experimental.pallas import tpu as pltpu
from jax.sharding import PartitionSpec as P

MESH = pl.DeviceIdType.MESH
STEPS = 128.0
TOP = 32640.0
PAD = 16


def encode(values, out):
    rows = values.shape[0]
    peak = jnp.maximum(jnp.max(jnp.abs(values), axis=0, keepdims=True), 2.0**-100)
    level = jnp.ceil(jnp.log2(peak) * STEPS + 0.5)
    factor = jnp.exp2(level * (-1.0 / STEPS)) * TOP
    coded = jnp.round(values * factor).astype(jnp.int32)
    out[0:rows, :] = coded.astype(jnp.int16)
    wide = jnp.broadcast_to(level, (PAD, values.shape[1]))
    out[rows : rows + PAD, :] = wide.astype(jnp.int32).astype(jnp.int16)


def decode(message, rows):
    level = message[rows : rows + PAD, :].astype(jnp.int32).astype(jnp.float32)[0:1, :]
    factor = jnp.exp2(level * (1.0 / STEPS)) * (1.0 / TOP)
    return message[0:rows, :].astype(jnp.int32).astype(jnp.float32) * factor


def kernel(sizes, widths, panel_hbm, in_hbm, slab_hbm, owner_hbm, out_hbm, out, *scratch):
    R, C, L = sizes
    N = len(widths)
    starts = [sum(widths[:n]) for n in range(N)]
    slabs, sbufs, rbufs = (scratch[i * N : (i + 1) * N] for i in range(3))
    ops, panel, in_pat, owner, out_pat, portion, acc, lp, ls, lm, sx, sc, sr, rp, ss, rs, sz, rz = scratch[3 * N :]
    H = C // 2
    row, col, z = lax.axis_index("row"), lax.axis_index("col"), lax.axis_index("layer")
    half, side = col // 2, col % 2
    mate = half * 2 + (1 - side)
    rows = out.shape[0]
    bs = slab_hbm.shape[2]
    depth = panel.shape[1]
    mine = slab_hbm.shape[1]
    brows = rows // bs
    hops = [((half + i) % H) * 2 + side for i in range(1, H)]
    relays = [((half + i) % H) * 2 + (1 - side) for i in range(1, H)]
    peers = [(row + i) % R for i in range(1, R)]

    barrier = pltpu.get_barrier_semaphore()
    for c in hops + [mate]:
        pl.semaphore_signal(barrier, inc=1, device_id={"col": c}, device_id_type=MESH)
    for r in peers:
        pl.semaphore_signal(barrier, inc=1, device_id={"row": r}, device_id_type=MESH)

    @pl.when(z > 0)
    def _():
        pl.semaphore_signal(barrier, inc=1, device_id={"layer": z - 1}, device_id_type=MESH)

    @pl.when(z < L - 1)
    def _():
        pl.semaphore_signal(barrier, inc=1, device_id={"layer": z + 1}, device_id_type=MESH)

    tables = [sorted(range(L), key=lambda d: (-abs(d - i), -i if d > i else i - L + 1)) for i in range(L)]

    def pick(t):
        found = 0
        for i in range(L):
            found = found + jnp.where(z == i, tables[i][t], 0)
        return found

    dest = [pick(t) for t in range(L)]

    def load_panel(t):
        here = pl.ds(pl.multiple_of(dest[t] * rows, rows), rows)
        return pltpu.make_async_copy(panel_hbm.at[here], panel.at[here], lp.at[t])

    def load_slab(n):
        return pltpu.make_async_copy(
            slab_hbm.at[0, :, :, pl.ds(starts[n], widths[n])], slabs[n].at[pl.ds(row * mine, mine)], ls.at[n])

    small = [
        pltpu.make_async_copy(src, dst, lm.at[i])
        for i, (src, dst) in enumerate([(in_hbm, in_pat), (owner_hbm, owner), (out_hbm, out_pat)])
    ]
    small[0].start()
    load_panel(0).start()
    load_slab(0).start()
    for t in range(1, max(L, N)):
        if t < L:
            load_panel(t).start()
        if t < N:
            load_slab(t).start()
    small[1].start()
    small[2].start()

    def mask(t):
        for i in range(brows):
            first = pl.multiple_of(dest[t] * rows + i * bs, bs)
            for j in range(depth // bs):
                keep = in_pat[j, dest[t] * brows + i].astype(jnp.float32)
                block = panel[pl.ds(first, bs), j * bs : (j + 1) * bs].astype(jnp.float32)
                portion[col, t, i * bs : (i + 1) * bs, j * bs : (j + 1) * bs] = (block * keep).astype(jnp.bfloat16)

    def send_part(c_to, t, sem):
        return pltpu.make_async_remote_copy(
            src_ref=portion.at[col, t], dst_ref=portion.at[col, t], send_sem=sem, recv_sem=rp.at[col, t],
            device_id={"col": c_to}, device_id_type=MESH)

    def relay(c_from, t, sem):
        return pltpu.make_async_remote_copy(
            src_ref=portion.at[c_from, t], dst_ref=portion.at[c_from, t], send_sem=sem, recv_sem=rp.at[c_from, t],
            device_id={"col": mate}, device_id_type=MESH)

    def send_slab(r_to, i, n):
        block = slabs[n].at[pl.ds(row * mine, mine)]
        return pltpu.make_async_remote_copy(
            src_ref=block, dst_ref=block, send_sem=ss.at[i, n], recv_sem=rs.at[row, n],
            device_id={"row": r_to}, device_id_type=MESH)

    def start_parts(t):
        for i, c in enumerate(hops):
            send_part(c, t, sx.at[i, t]).start()
        send_part(mate, t, sc.at[t]).start()

    def start_slab(n):
        for i, r in enumerate(peers):
            send_slab(r, i, n).start()

    small[0].wait()
    load_panel(0).wait()
    mask(0)
    load_slab(0).wait()
    pl.semaphore_wait(barrier, (R - 1) + H + jnp.where(z > 0, 1, 0) + jnp.where(z < L - 1, 1, 0))
    start_slab(0)
    start_parts(0)
    for t in range(1, max(L, N)):
        if t < N:
            load_slab(t).wait()
            start_slab(t)
        if t < L:
            load_panel(t).wait()
            mask(t)
            start_parts(t)
    small[1].wait()
    small[2].wait()

    def ready_parts(t):
        for i, c in enumerate(hops):
            relay(c, t, sr.at[i, t]).wait_recv()
            relay(c, t, sr.at[i, t]).start()

    def wait_parts(t):
        for c in [mate] + relays:
            relay(c, t, sc.at[t]).wait_recv()

    def ready_slab(n):
        for r in peers:
            pltpu.make_async_remote_copy(
                src_ref=slabs[n].at[pl.ds(r * mine, mine)], dst_ref=slabs[n].at[pl.ds(r * mine, mine)],
                send_sem=ss.at[0, n], recv_sem=rs.at[r, n], device_id={"row": r}, device_id_type=MESH).wait_recv()
        for j in range(R * mine):
            ops[j * bs : (j + 1) * bs, starts[n] : starts[n] + widths[n]] = slabs[n][owner[0, j]]

    near = min(2, L - 1)

    def product(t, n):
        left = jnp.concatenate([portion[c, t] for c in range(C)], axis=1)
        return jnp.dot(left, ops[:, starts[n] : starts[n] + widths[n]], preferred_element_type=jnp.float32)

    def multiply_near():
        left = [portion[c, near:L].reshape((L - near) * rows, depth) for c in range(C)]
        acc[...] = jnp.dot(jnp.concatenate(left, axis=1), ops[...], preferred_element_type=jnp.float32)

    def message(t, n, slot, to):
        return pltpu.make_async_remote_copy(
            src_ref=sbufs[n].at[t], dst_ref=rbufs[n].at[slot], send_sem=sz.at[t, n], recv_sem=rz.at[slot, n],
            device_id={"layer": to}, device_id_type=MESH)

    def arrived(slot, n):
        message(0, n, slot, (z + 1) % L).wait_recv()
        return decode(rbufs[n].at[slot], rows)

    def route(t):
        up = jnp.where(dest[t] > z, 1, 0)
        return dest[t] + L * (1 - up), z + 2 * up - 1

    inner = (z > 0) & (z < L - 1)

    def pass_on(t, n, add):
        slot, to = route(t)
        if t < near:
            total = product(t, n)
        else:
            total = acc[(t - near) * rows : (t - near + 1) * rows, starts[n] : starts[n] + widths[n]]
        if add:
            total = total + arrived(slot, n)
        encode(total, sbufs[n].at[t])
        message(t, n, slot, to).start()

    def parts(*steps):
        for t in steps:
            ready_parts(t)
        for t in steps:
            wait_parts(t)

    def finish(n, up, down):
        here = slice(starts[n], starts[n] + widths[n])
        total = acc[(L - 1 - near) * rows :, here]
        if up:
            total = total + arrived(z, n)
        if down:
            total = total + arrived(z + L, n)
        for i in range(brows):
            for j in range(widths[n] // bs):
                keep = out_pat[i, starts[n] // bs + j].astype(jnp.float32)
                block = total[i * bs : (i + 1) * bs, j * bs : (j + 1) * bs] * keep
                first = starts[n] + j * bs
                out[i * bs : (i + 1) * bs, first : first + bs] = block.astype(jnp.bfloat16)

    late = list(range(near, L))
    tail = [(t, n) for t in range(2, L - 1) for n in range(N)]

    @pl.when(jnp.logical_not(inner))
    def _():
        for n in range(N):
            if n == 0:
                ready_parts(0)
            ready_slab(n)
            if n == 0:
                wait_parts(0)
            pass_on(0, n, False)
            if n == 1 and near > 1:
                parts(1)
                pass_on(1, 0, False)
            if n > 0 and near > 1:
                pass_on(1, n, False)
        parts(*late)
        multiply_near()
        for t, n in tail:
            pass_on(t, n, False)

        @pl.when(z > 0)
        def _():
            for n in range(N):
                finish(n, True, False)

        @pl.when(z == 0)
        def _():
            for n in range(N):
                finish(n, False, L > 1)

    if L > 2:

        @pl.when(inner)
        def _():
            for n in range(N):
                if n == 0:
                    ready_parts(0)
                ready_slab(n)
                if n == 0:
                    wait_parts(0)
                if n == N - 1:
                    parts(*late)
                    multiply_near()
                    if N > 2:
                        pass_on(1, N - 3, True)
                pass_on(0, n, True)
                if n == 0:
                    parts(1)
                elif n < N - 1 and n > 1:
                    pass_on(1, n - 2, True)
            order = [(1, n) for n in range(max(N - 2, 0), N)]
            for i, (t, n) in enumerate(tail):
                if i < len(order):
                    pass_on(*order[i], True)
                pass_on(t, n, True)
            for t, n in order[len(tail) :]:
                pass_on(t, n, True)
            for n in range(N):
                finish(n, True, True)

    for t in range(L):
        for i, c in enumerate(hops):
            send_part(c, t, sx.at[i, t]).wait_send()
            relay(c, t, sr.at[i, t]).wait_send()
        send_part(mate, t, sc.at[t]).wait_send()
    for n in range(N):
        for i, r in enumerate(peers):
            send_slab(r, i, n).wait_send()
        for t in range(L - 1):
            slot, to = route(t)
            message(t, n, slot, to).wait_send()


def solution(mesh):
    R, C, L = (mesh.shape[name] for name in ("row", "col", "layer"))

    def shards(panel, in_pat, slab, owner, out_pat):
        bs, cols = slab.shape[2], slab.shape[3]
        rows = panel.shape[0] // L
        depth = panel.shape[2]
        blocks = R * slab.shape[1]
        widths = (cols // 4,) * 4
        N = len(widths)
        H = C // 2
        dma = pltpu.SemaphoreType.DMA
        vmem = pl.BlockSpec(memory_space=pltpu.VMEM)
        hbm = pl.BlockSpec(memory_space=pltpu.HBM)
        return pl.pallas_call(
            functools.partial(kernel, (R, C, L), widths),
            out_shape=jax.ShapeDtypeStruct((rows, cols), jnp.bfloat16),
            in_specs=[hbm] * 5,
            out_specs=vmem,
            scratch_shapes=[pltpu.VMEM((blocks, bs, w), jnp.bfloat16) for w in widths]
            + [pltpu.VMEM((L - 1, rows + PAD, w), jnp.int16) for w in widths]
            + [pltpu.VMEM((2 * L, rows + PAD, w), jnp.int16) for w in widths]
            + [
                pltpu.VMEM((blocks * bs, cols), jnp.bfloat16),
                pltpu.VMEM((panel.shape[0], depth), jnp.bfloat16),
                pltpu.SMEM((in_pat.shape[2], in_pat.shape[0]), jnp.int32),
                pltpu.SMEM(owner.shape, jnp.int32),
                pltpu.SMEM(out_pat.shape, jnp.int32),
                pltpu.VMEM((C, L, rows, depth), jnp.bfloat16),
                pltpu.VMEM(((L - min(2, L - 1)) * rows, cols), jnp.float32),
                dma((L,)),
                dma((N,)),
                dma((3,)),
                dma((H - 1, L)),
                dma((L,)),
                dma((H - 1, L)),
                dma((C, L)),
                dma((R - 1, N)),
                dma((R, N)),
                dma((L - 1, N)),
                dma((2 * L, N)),
            ],
            compiler_params=pltpu.CompilerParams(
                collective_id=0, has_side_effects=True, vmem_limit_bytes=56 * 2**20),
        )(panel.reshape(panel.shape[0], depth), in_pat[:, 0, :].T, slab, owner, out_pat)

    in_specs = (
        P("row", "layer", "col"),
        P("row", "layer", "col"),
        P("layer", "row", None, "col"),
        P("layer", None),
        P(("row", "layer"), "col"),
    )
    out_specs = P(("row", "layer"), "col")
    return jax.shard_map(shards, mesh=mesh, in_specs=in_specs, out_specs=out_specs, check_vma=False)
```

```python
import functools

import jax
import jax.numpy as jnp
from jax import lax
from jax.experimental import pallas as pl
from jax.experimental.pallas import tpu as pltpu
from jax.sharding import PartitionSpec as P

MESH = pl.DeviceIdType.MESH
STEPS = 128.0
TOP = 32640.0
PAD = 16


def encode(values, out):
    rows = values.shape[0]
    peak = jnp.maximum(jnp.max(jnp.abs(values), axis=0, keepdims=True), 2.0**-100)
    level = jnp.ceil(jnp.log2(peak) * STEPS + 0.5)
    factor = jnp.exp2(level * (-1.0 / STEPS)) * TOP
    coded = jnp.round(values * factor).astype(jnp.int32)
    out[0:rows, :] = coded.astype(jnp.int16)
    wide = jnp.broadcast_to(level, (PAD, values.shape[1]))
    out[rows : rows + PAD, :] = wide.astype(jnp.int32).astype(jnp.int16)


def decode(message, rows):
    level = message[rows : rows + PAD, :].astype(jnp.int32).astype(jnp.float32)[0:1, :]
    factor = jnp.exp2(level * (1.0 / STEPS)) * (1.0 / TOP)
    return message[0:rows, :].astype(jnp.int32).astype(jnp.float32) * factor


def kernel(sizes, widths, panel_hbm, in_hbm, slab_hbm, owner_hbm, out_hbm, out, *scratch):
    R, C, L = sizes
    N = len(widths)
    starts = [sum(widths[:n]) for n in range(N)]
    slabs, sbufs, rbufs = (scratch[i * N : (i + 1) * N] for i in range(3))
    ops, panel, in_pat, owner, out_pat, portion, acc, lp, ls, lm, sx, sc, sr, rp, ss, rs, sz, rz = scratch[3 * N :]
    H = C // 2
    row, col, z = lax.axis_index("row"), lax.axis_index("col"), lax.axis_index("layer")
    half, side = col // 2, col % 2
    mate = half * 2 + (1 - side)
    rows = out.shape[0]
    bs = slab_hbm.shape[2]
    depth = panel.shape[1]
    mine = slab_hbm.shape[1]
    brows = rows // bs
    hops = [((half + i) % H) * 2 + side for i in range(1, H)]
    relays = [((half + i) % H) * 2 + (1 - side) for i in range(1, H)]
    peers = [(row + i) % R for i in range(1, R)]

    barrier = pltpu.get_barrier_semaphore()
    for c in hops + [mate]:
        pl.semaphore_signal(barrier, inc=1, device_id={"col": c}, device_id_type=MESH)
    for r in peers:
        pl.semaphore_signal(barrier, inc=1, device_id={"row": r}, device_id_type=MESH)

    @pl.when(z > 0)
    def _():
        pl.semaphore_signal(barrier, inc=1, device_id={"layer": z - 1}, device_id_type=MESH)

    @pl.when(z < L - 1)
    def _():
        pl.semaphore_signal(barrier, inc=1, device_id={"layer": z + 1}, device_id_type=MESH)

    tables = [sorted(range(L), key=lambda d: (-abs(d - i), -i if d > i else i - L + 1)) for i in range(L)]

    def pick(t):
        found = 0
        for i in range(L):
            found = found + jnp.where(z == i, tables[i][t], 0)
        return found

    dest = [pick(t) for t in range(L)]

    def load_panel(t):
        here = pl.ds(pl.multiple_of(dest[t] * rows, rows), rows)
        return pltpu.make_async_copy(panel_hbm.at[here], panel.at[here], lp.at[t])

    def load_slab(n):
        return pltpu.make_async_copy(
            slab_hbm.at[0, :, :, pl.ds(starts[n], widths[n])], slabs[n].at[pl.ds(row * mine, mine)], ls.at[n])

    small = [
        pltpu.make_async_copy(src, dst, lm.at[i])
        for i, (src, dst) in enumerate([(in_hbm, in_pat), (owner_hbm, owner), (out_hbm, out_pat)])
    ]
    small[0].start()
    load_panel(0).start()
    load_slab(0).start()
    for t in range(1, max(L, N)):
        if t < L:
            load_panel(t).start()
        if t < N:
            load_slab(t).start()
    small[1].start()
    small[2].start()

    def mask(t):
        for i in range(brows):
            first = pl.multiple_of(dest[t] * rows + i * bs, bs)
            for j in range(depth // bs):
                keep = in_pat[j, dest[t] * brows + i].astype(jnp.float32)
                block = panel[pl.ds(first, bs), j * bs : (j + 1) * bs].astype(jnp.float32)
                portion[col, t, i * bs : (i + 1) * bs, j * bs : (j + 1) * bs] = (block * keep).astype(jnp.bfloat16)

    def send_part(c_to, t, sem):
        return pltpu.make_async_remote_copy(
            src_ref=portion.at[col, t], dst_ref=portion.at[col, t], send_sem=sem, recv_sem=rp.at[col, t],
            device_id={"col": c_to}, device_id_type=MESH)

    def relay(c_from, t, sem):
        return pltpu.make_async_remote_copy(
            src_ref=portion.at[c_from, t], dst_ref=portion.at[c_from, t], send_sem=sem, recv_sem=rp.at[c_from, t],
            device_id={"col": mate}, device_id_type=MESH)

    def send_slab(r_to, i, n):
        block = slabs[n].at[pl.ds(row * mine, mine)]
        return pltpu.make_async_remote_copy(
            src_ref=block, dst_ref=block, send_sem=ss.at[i, n], recv_sem=rs.at[row, n],
            device_id={"row": r_to}, device_id_type=MESH)

    def start_parts(t):
        for i, c in enumerate(hops):
            send_part(c, t, sx.at[i, t]).start()
        send_part(mate, t, sc.at[t]).start()

    def start_slab(n):
        for i, r in enumerate(peers):
            send_slab(r, i, n).start()

    small[0].wait()
    load_panel(0).wait()
    mask(0)
    load_slab(0).wait()
    pl.semaphore_wait(barrier, (R - 1) + H + jnp.where(z > 0, 1, 0) + jnp.where(z < L - 1, 1, 0))
    start_slab(0)
    start_parts(0)
    for t in range(1, max(L, N)):
        if t < N:
            load_slab(t).wait()
            start_slab(t)
        if t < L:
            load_panel(t).wait()
            mask(t)
            start_parts(t)
    small[1].wait()
    small[2].wait()

    def ready_parts(t):
        for i, c in enumerate(hops):
            relay(c, t, sr.at[i, t]).wait_recv()
            relay(c, t, sr.at[i, t]).start()

    def wait_parts(t):
        for c in [mate] + relays:
            relay(c, t, sc.at[t]).wait_recv()

    def ready_slab(n):
        for r in peers:
            pltpu.make_async_remote_copy(
                src_ref=slabs[n].at[pl.ds(r * mine, mine)], dst_ref=slabs[n].at[pl.ds(r * mine, mine)],
                send_sem=ss.at[0, n], recv_sem=rs.at[r, n], device_id={"row": r}, device_id_type=MESH).wait_recv()
        for j in range(R * mine):
            ops[j * bs : (j + 1) * bs, starts[n] : starts[n] + widths[n]] = slabs[n][owner[0, j]]

    near = min(2, L - 1)

    def product(t, n):
        left = jnp.concatenate([portion[c, t] for c in range(C)], axis=1)
        return jnp.dot(left, ops[:, starts[n] : starts[n] + widths[n]], preferred_element_type=jnp.float32)

    def multiply_from(t):
        left = [portion[c, t:L].reshape((L - t) * rows, depth) for c in range(C)]
        acc[(t - near) * rows :, :] = jnp.dot(jnp.concatenate(left, axis=1), ops[...], preferred_element_type=jnp.float32)

    def message(t, n, slot, to):
        return pltpu.make_async_remote_copy(
            src_ref=sbufs[n].at[t], dst_ref=rbufs[n].at[slot], send_sem=sz.at[t, n], recv_sem=rz.at[slot, n],
            device_id={"layer": to}, device_id_type=MESH)

    def arrived(slot, n):
        message(0, n, slot, (z + 1) % L).wait_recv()
        return decode(rbufs[n].at[slot], rows)

    def route(t):
        up = jnp.where(dest[t] > z, 1, 0)
        return dest[t] + L * (1 - up), z + 2 * up - 1

    inner = (z > 0) & (z < L - 1)

    def pass_on(t, n, add):
        slot, to = route(t)
        if add or t < near:
            total = product(t, n)
        else:
            total = acc[(t - near) * rows : (t - near + 1) * rows, starts[n] : starts[n] + widths[n]]
        if add:
            total = total + arrived(slot, n)
        encode(total, sbufs[n].at[t])
        message(t, n, slot, to).start()

    def parts(*steps):
        for t in steps:
            ready_parts(t)
        for t in steps:
            wait_parts(t)

    def finish(n, up, down):
        here = slice(starts[n], starts[n] + widths[n])
        total = acc[(L - 1 - near) * rows :, here]
        if up:
            total = total + arrived(z, n)
        if down:
            total = total + arrived(z + L, n)
        for i in range(brows):
            for j in range(widths[n] // bs):
                keep = out_pat[i, starts[n] // bs + j].astype(jnp.float32)
                block = total[i * bs : (i + 1) * bs, j * bs : (j + 1) * bs] * keep
                first = starts[n] + j * bs
                out[i * bs : (i + 1) * bs, first : first + bs] = block.astype(jnp.bfloat16)

    late = list(range(near, L))
    tail = [(t, n) for t in range(2, L - 1) for n in range(N)]

    @pl.when(jnp.logical_not(inner))
    def _():
        for n in range(N):
            if n == 0:
                ready_parts(0)
            ready_slab(n)
            if n == 0:
                wait_parts(0)
            pass_on(0, n, False)
            if n == 1 and near > 1:
                parts(1)
                pass_on(1, 0, False)
            if n > 0 and near > 1:
                pass_on(1, n, False)
        parts(*late)
        multiply_from(near)
        for t, n in tail:
            pass_on(t, n, False)

        @pl.when(z > 0)
        def _():
            for n in range(N):
                finish(n, True, False)

        @pl.when(z == 0)
        def _():
            for n in range(N):
                finish(n, False, L > 1)

    if L > 2:

        @pl.when(inner)
        def _():
            for n in range(N):
                if n == 0:
                    ready_parts(0)
                ready_slab(n)
                if n == 0:
                    wait_parts(0)
                elif n < L - 1:
                    parts(n)
                pass_on(0, n, True)
                if n == N - 1:
                    parts(*range(N, L - 1))
                elif n < 2:
                    continue
                first = 0 if n == min(2, N - 1) else n - 1
                for m in range(first, min(n, N - 1)):
                    for t in range(1, L - 1):
                        pass_on(t, m, True)
            parts(L - 1)
            multiply_from(L - 1)
            for t in range(1, L - 1):
                pass_on(t, N - 1, True)
            for n in range(N):
                finish(n, True, True)

    for t in range(L):
        for i, c in enumerate(hops):
            send_part(c, t, sx.at[i, t]).wait_send()
            relay(c, t, sr.at[i, t]).wait_send()
        send_part(mate, t, sc.at[t]).wait_send()
    for n in range(N):
        for i, r in enumerate(peers):
            send_slab(r, i, n).wait_send()
        for t in range(L - 1):
            slot, to = route(t)
            message(t, n, slot, to).wait_send()


def solution(mesh):
    R, C, L = (mesh.shape[name] for name in ("row", "col", "layer"))

    def shards(panel, in_pat, slab, owner, out_pat):
        bs, cols = slab.shape[2], slab.shape[3]
        rows = panel.shape[0] // L
        depth = panel.shape[2]
        blocks = R * slab.shape[1]
        widths = (cols // 4,) * 4
        N = len(widths)
        H = C // 2
        dma = pltpu.SemaphoreType.DMA
        vmem = pl.BlockSpec(memory_space=pltpu.VMEM)
        hbm = pl.BlockSpec(memory_space=pltpu.HBM)
        return pl.pallas_call(
            functools.partial(kernel, (R, C, L), widths),
            out_shape=jax.ShapeDtypeStruct((rows, cols), jnp.bfloat16),
            in_specs=[hbm] * 5,
            out_specs=vmem,
            scratch_shapes=[pltpu.VMEM((blocks, bs, w), jnp.bfloat16) for w in widths]
            + [pltpu.VMEM((L - 1, rows + PAD, w), jnp.int16) for w in widths]
            + [pltpu.VMEM((2 * L, rows + PAD, w), jnp.int16) for w in widths]
            + [
                pltpu.VMEM((blocks * bs, cols), jnp.bfloat16),
                pltpu.VMEM((panel.shape[0], depth), jnp.bfloat16),
                pltpu.SMEM((in_pat.shape[2], in_pat.shape[0]), jnp.int32),
                pltpu.SMEM(owner.shape, jnp.int32),
                pltpu.SMEM(out_pat.shape, jnp.int32),
                pltpu.VMEM((C, L, rows, depth), jnp.bfloat16),
                pltpu.VMEM(((L - min(2, L - 1)) * rows, cols), jnp.float32),
                dma((L,)),
                dma((N,)),
                dma((3,)),
                dma((H - 1, L)),
                dma((L,)),
                dma((H - 1, L)),
                dma((C, L)),
                dma((R - 1, N)),
                dma((R, N)),
                dma((L - 1, N)),
                dma((2 * L, N)),
            ],
            compiler_params=pltpu.CompilerParams(
                collective_id=0, has_side_effects=True, vmem_limit_bytes=56 * 2**20),
        )(panel.reshape(panel.shape[0], depth), in_pat[:, 0, :].T, slab, owner, out_pat)

    in_specs = (
        P("row", "layer", "col"),
        P("row", "layer", "col"),
        P("layer", "row", None, "col"),
        P("layer", None),
        P(("row", "layer"), "col"),
    )
    out_specs = P(("row", "layer"), "col")
    return jax.shard_map(shards, mesh=mesh, in_specs=in_specs, out_specs=out_specs, check_vma=False)
```

```python
import functools

import jax
import jax.numpy as jnp
from jax import lax
from jax.experimental import pallas as pl
from jax.experimental.pallas import tpu as pltpu
from jax.sharding import PartitionSpec as P

MESH = pl.DeviceIdType.MESH
STEPS = 128.0
TOP = 32640.0
PAD = 16


def encode(values, out):
    rows = values.shape[0]
    peak = jnp.maximum(jnp.max(jnp.abs(values), axis=0, keepdims=True), 2.0**-100)
    level = jnp.ceil(jnp.log2(peak) * STEPS + 0.5)
    factor = jnp.exp2(level * (-1.0 / STEPS)) * TOP
    coded = jnp.round(values * factor).astype(jnp.int32)
    out[0:rows, :] = coded.astype(jnp.int16)
    wide = jnp.broadcast_to(level, (PAD, values.shape[1]))
    out[rows : rows + PAD, :] = wide.astype(jnp.int32).astype(jnp.int16)


def decode(message, rows):
    level = message[rows : rows + PAD, :].astype(jnp.int32).astype(jnp.float32)[0:1, :]
    factor = jnp.exp2(level * (1.0 / STEPS)) * (1.0 / TOP)
    return message[0:rows, :].astype(jnp.int32).astype(jnp.float32) * factor


def kernel(sizes, widths, panel_hbm, in_hbm, slab_hbm, owner_hbm, out_hbm, out, *scratch):
    R, C, L = sizes
    N = len(widths)
    starts = [sum(widths[:n]) for n in range(N)]
    slabs, sbufs, rbufs = (scratch[i * N : (i + 1) * N] for i in range(3))
    ops, panel, in_pat, owner, out_pat, portion, acc, lp, ls, lm, sx, sc, sr, rp, ss, rs, sz, rz = scratch[3 * N :]
    H = C // 2
    row, col, z = lax.axis_index("row"), lax.axis_index("col"), lax.axis_index("layer")
    half, side = col // 2, col % 2
    mate = half * 2 + (1 - side)
    rows = out.shape[0]
    bs = slab_hbm.shape[2]
    depth = panel.shape[1]
    mine = slab_hbm.shape[1]
    brows = rows // bs
    hops = [((half + i) % H) * 2 + side for i in range(1, H)]
    relays = [((half + i) % H) * 2 + (1 - side) for i in range(1, H)]
    peers = [(row + i) % R for i in range(1, R)]

    barrier = pltpu.get_barrier_semaphore()
    for c in hops + [mate]:
        pl.semaphore_signal(barrier, inc=1, device_id={"col": c}, device_id_type=MESH)
    for r in peers:
        pl.semaphore_signal(barrier, inc=1, device_id={"row": r}, device_id_type=MESH)

    @pl.when(z > 0)
    def _():
        pl.semaphore_signal(barrier, inc=1, device_id={"layer": z - 1}, device_id_type=MESH)

    @pl.when(z < L - 1)
    def _():
        pl.semaphore_signal(barrier, inc=1, device_id={"layer": z + 1}, device_id_type=MESH)

    tables = [sorted(range(L), key=lambda d: (-abs(d - i), -i if d > i else i - L + 1)) for i in range(L)]

    def pick(t):
        found = 0
        for i in range(L):
            found = found + jnp.where(z == i, tables[i][t], 0)
        return found

    dest = [pick(t) for t in range(L)]

    def load_panel(t):
        here = pl.ds(pl.multiple_of(dest[t] * rows, rows), rows)
        return pltpu.make_async_copy(panel_hbm.at[here], panel.at[here], lp.at[t])

    def load_slab(n):
        return pltpu.make_async_copy(
            slab_hbm.at[0, :, :, pl.ds(starts[n], widths[n])], slabs[n].at[pl.ds(row * mine, mine)], ls.at[n])

    small = [
        pltpu.make_async_copy(src, dst, lm.at[i])
        for i, (src, dst) in enumerate([(in_hbm, in_pat), (owner_hbm, owner), (out_hbm, out_pat)])
    ]
    small[0].start()
    load_panel(0).start()
    load_slab(0).start()
    for t in range(1, max(L, N)):
        if t < L:
            load_panel(t).start()
        if t < N:
            load_slab(t).start()
    small[1].start()
    small[2].start()

    def mask(t):
        for i in range(brows):
            first = pl.multiple_of(dest[t] * rows + i * bs, bs)
            for j in range(depth // bs):
                keep = in_pat[j, dest[t] * brows + i].astype(jnp.float32)
                block = panel[pl.ds(first, bs), j * bs : (j + 1) * bs].astype(jnp.float32)
                portion[col, t, i * bs : (i + 1) * bs, j * bs : (j + 1) * bs] = (block * keep).astype(jnp.bfloat16)

    def send_part(c_to, t, sem):
        return pltpu.make_async_remote_copy(
            src_ref=portion.at[col, t], dst_ref=portion.at[col, t], send_sem=sem, recv_sem=rp.at[col, t],
            device_id={"col": c_to}, device_id_type=MESH)

    def relay(c_from, t, sem):
        return pltpu.make_async_remote_copy(
            src_ref=portion.at[c_from, t], dst_ref=portion.at[c_from, t], send_sem=sem, recv_sem=rp.at[c_from, t],
            device_id={"col": mate}, device_id_type=MESH)

    def send_slab(r_to, i, n):
        block = slabs[n].at[pl.ds(row * mine, mine)]
        return pltpu.make_async_remote_copy(
            src_ref=block, dst_ref=block, send_sem=ss.at[i, n], recv_sem=rs.at[row, n],
            device_id={"row": r_to}, device_id_type=MESH)

    def start_parts(t):
        for i, c in enumerate(hops):
            send_part(c, t, sx.at[i, t]).start()
        send_part(mate, t, sc.at[t]).start()

    def start_slab(n):
        for i, r in enumerate(peers):
            send_slab(r, i, n).start()

    small[0].wait()
    load_panel(0).wait()
    mask(0)
    load_slab(0).wait()
    pl.semaphore_wait(barrier, (R - 1) + H + jnp.where(z > 0, 1, 0) + jnp.where(z < L - 1, 1, 0))
    start_slab(0)
    start_parts(0)
    for t in range(1, max(L, N)):
        if t < N:
            load_slab(t).wait()
            start_slab(t)
        if t < L:
            load_panel(t).wait()
            mask(t)
            start_parts(t)
    small[1].wait()
    small[2].wait()

    def ready_parts(t):
        for i, c in enumerate(hops):
            relay(c, t, sr.at[i, t]).wait_recv()
            relay(c, t, sr.at[i, t]).start()

    def wait_parts(t):
        for c in [mate] + relays:
            relay(c, t, sc.at[t]).wait_recv()

    def ready_slab(n):
        for r in peers:
            pltpu.make_async_remote_copy(
                src_ref=slabs[n].at[pl.ds(r * mine, mine)], dst_ref=slabs[n].at[pl.ds(r * mine, mine)],
                send_sem=ss.at[0, n], recv_sem=rs.at[r, n], device_id={"row": r}, device_id_type=MESH).wait_recv()
        for j in range(R * mine):
            ops[j * bs : (j + 1) * bs, starts[n] : starts[n] + widths[n]] = slabs[n][owner[0, j]]

    near = min(2, L - 1)

    def product(t, n):
        left = jnp.concatenate([portion[c, t] for c in range(C)], axis=1)
        return jnp.dot(left, ops[:, starts[n] : starts[n] + widths[n]], preferred_element_type=jnp.float32)

    def multiply_from(t):
        left = [portion[c, t:L].reshape((L - t) * rows, depth) for c in range(C)]
        acc[(t - near) * rows :, :] = jnp.dot(jnp.concatenate(left, axis=1), ops[...], preferred_element_type=jnp.float32)

    def message(t, n, slot, to):
        return pltpu.make_async_remote_copy(
            src_ref=sbufs[n].at[t], dst_ref=rbufs[n].at[slot], send_sem=sz.at[t, n], recv_sem=rz.at[slot, n],
            device_id={"layer": to}, device_id_type=MESH)

    def arrived(slot, n):
        message(0, n, slot, (z + 1) % L).wait_recv()
        return decode(rbufs[n].at[slot], rows)

    def route(t):
        up = jnp.where(dest[t] > z, 1, 0)
        return dest[t] + L * (1 - up), z + 2 * up - 1

    inner = (z > 0) & (z < L - 1)

    def pass_on(t, n, add):
        slot, to = route(t)
        if add or t < near:
            total = product(t, n)
        else:
            total = acc[(t - near) * rows : (t - near + 1) * rows, starts[n] : starts[n] + widths[n]]
        if add:
            total = total + arrived(slot, n)
        encode(total, sbufs[n].at[t])
        message(t, n, slot, to).start()

    def parts(*steps):
        for t in steps:
            ready_parts(t)
        for t in steps:
            wait_parts(t)

    def finish(n, up, down):
        here = slice(starts[n], starts[n] + widths[n])
        total = acc[(L - 1 - near) * rows :, here]
        if up:
            total = total + arrived(z, n)
        if down:
            total = total + arrived(z + L, n)
        for i in range(brows):
            for j in range(widths[n] // bs):
                keep = out_pat[i, starts[n] // bs + j].astype(jnp.float32)
                block = total[i * bs : (i + 1) * bs, j * bs : (j + 1) * bs] * keep
                first = starts[n] + j * bs
                out[i * bs : (i + 1) * bs, first : first + bs] = block.astype(jnp.bfloat16)

    late = list(range(near, L))
    tail = [(t, n) for t in range(2, L - 1) for n in range(N)]

    @pl.when(jnp.logical_not(inner))
    def _():
        for n in range(N):
            if n == 0:
                ready_parts(0)
            ready_slab(n)
            if n == 0:
                wait_parts(0)
            pass_on(0, n, False)
            if n == 1 and near > 1:
                parts(1)
            if near > 1:
                for m in {1: (0, 1), N - 1: range(2, N)}.get(n, ()):
                    pass_on(1, m, False)
        parts(*late)
        multiply_from(near)
        for t, n in tail:
            pass_on(t, n, False)

        @pl.when(z > 0)
        def _():
            for n in range(N):
                finish(n, True, False)

        @pl.when(z == 0)
        def _():
            for n in range(N):
                finish(n, False, L > 1)

    if L > 2:

        @pl.when(inner)
        def _():
            for n in range(N):
                if n == 0:
                    ready_parts(0)
                ready_slab(n)
                if n == 0:
                    wait_parts(0)
                elif n < L:
                    parts(n)
                if n == N - 1:
                    parts(*range(N, L))
                    pass_on(1, n - 1, True)
                    multiply_from(L - 1)
                pass_on(0, n, True)
                if n == N - 2:
                    for m in range(n):
                        for t in range(1, L - 1):
                            pass_on(t, m, True)
            pass_on(1, N - 1, True)
            for n in (N - 2, N - 1):
                for t in range(2, L - 1):
                    pass_on(t, n, True)
            for n in range(N):
                finish(n, True, True)

    for t in range(L):
        for i, c in enumerate(hops):
            send_part(c, t, sx.at[i, t]).wait_send()
            relay(c, t, sr.at[i, t]).wait_send()
        send_part(mate, t, sc.at[t]).wait_send()
    for n in range(N):
        for i, r in enumerate(peers):
            send_slab(r, i, n).wait_send()
        for t in range(L - 1):
            slot, to = route(t)
            message(t, n, slot, to).wait_send()


def solution(mesh):
    R, C, L = (mesh.shape[name] for name in ("row", "col", "layer"))

    def shards(panel, in_pat, slab, owner, out_pat):
        bs, cols = slab.shape[2], slab.shape[3]
        rows = panel.shape[0] // L
        depth = panel.shape[2]
        blocks = R * slab.shape[1]
        widths = (cols // 4,) * 4
        N = len(widths)
        H = C // 2
        dma = pltpu.SemaphoreType.DMA
        vmem = pl.BlockSpec(memory_space=pltpu.VMEM)
        hbm = pl.BlockSpec(memory_space=pltpu.HBM)
        return pl.pallas_call(
            functools.partial(kernel, (R, C, L), widths),
            out_shape=jax.ShapeDtypeStruct((rows, cols), jnp.bfloat16),
            in_specs=[hbm] * 5,
            out_specs=vmem,
            scratch_shapes=[pltpu.VMEM((blocks, bs, w), jnp.bfloat16) for w in widths]
            + [pltpu.VMEM((L - 1, rows + PAD, w), jnp.int16) for w in widths]
            + [pltpu.VMEM((2 * L, rows + PAD, w), jnp.int16) for w in widths]
            + [
                pltpu.VMEM((blocks * bs, cols), jnp.bfloat16),
                pltpu.VMEM((panel.shape[0], depth), jnp.bfloat16),
                pltpu.SMEM((in_pat.shape[2], in_pat.shape[0]), jnp.int32),
                pltpu.SMEM(owner.shape, jnp.int32),
                pltpu.SMEM(out_pat.shape, jnp.int32),
                pltpu.VMEM((C, L, rows, depth), jnp.bfloat16),
                pltpu.VMEM(((L - min(2, L - 1)) * rows, cols), jnp.float32),
                dma((L,)),
                dma((N,)),
                dma((3,)),
                dma((H - 1, L)),
                dma((L,)),
                dma((H - 1, L)),
                dma((C, L)),
                dma((R - 1, N)),
                dma((R, N)),
                dma((L - 1, N)),
                dma((2 * L, N)),
            ],
            compiler_params=pltpu.CompilerParams(
                collective_id=0, has_side_effects=True, vmem_limit_bytes=56 * 2**20),
        )(panel.reshape(panel.shape[0], depth), in_pat[:, 0, :].T, slab, owner, out_pat)

    in_specs = (
        P("row", "layer", "col"),
        P("row", "layer", "col"),
        P("layer", "row", None, "col"),
        P("layer", None),
        P(("row", "layer"), "col"),
    )
    out_specs = P(("row", "layer"), "col")
    return jax.shard_map(shards, mesh=mesh, in_specs=in_specs, out_specs=out_specs, check_vma=False)
```

```python
import functools

import jax
import jax.numpy as jnp
from jax import lax
from jax.experimental import pallas as pl
from jax.experimental.pallas import tpu as pltpu
from jax.sharding import PartitionSpec as P

MESH = pl.DeviceIdType.MESH
STEPS = 128.0
TOP = 32640.0
PAD = 16


def encode(values, out):
    rows = values.shape[0]
    peak = jnp.maximum(jnp.max(jnp.abs(values), axis=0, keepdims=True), 2.0**-100)
    level = jnp.ceil(jnp.log2(peak) * STEPS + 0.5)
    factor = jnp.exp2(level * (-1.0 / STEPS)) * TOP
    coded = jnp.round(values * factor).astype(jnp.int32)
    out[0:rows, :] = coded.astype(jnp.int16)
    wide = jnp.broadcast_to(level, (PAD, values.shape[1]))
    out[rows : rows + PAD, :] = wide.astype(jnp.int32).astype(jnp.int16)


def decode(message, rows):
    level = message[rows : rows + PAD, :].astype(jnp.int32).astype(jnp.float32)[0:1, :]
    factor = jnp.exp2(level * (1.0 / STEPS)) * (1.0 / TOP)
    return message[0:rows, :].astype(jnp.int32).astype(jnp.float32) * factor


def kernel(sizes, widths, panel_hbm, in_hbm, slab_hbm, owner_hbm, out_hbm, out, *scratch):
    R, C, L = sizes
    N = len(widths)
    starts = [sum(widths[:n]) for n in range(N)]
    slabs, sbufs, rbufs = (scratch[i * N : (i + 1) * N] for i in range(3))
    ops, panel, in_pat, owner, out_pat, portion, acc, lp, ls, lm, sx, sc, sr, rp, ss, rs, sz, rz = scratch[3 * N :]
    H = C // 2
    row, col, z = lax.axis_index("row"), lax.axis_index("col"), lax.axis_index("layer")
    half, side = col // 2, col % 2
    mate = half * 2 + (1 - side)
    rows = out.shape[0]
    bs = slab_hbm.shape[2]
    depth = panel.shape[1]
    mine = slab_hbm.shape[1]
    brows = rows // bs
    hops = [((half + i) % H) * 2 + side for i in range(1, H)]
    relays = [((half + i) % H) * 2 + (1 - side) for i in range(1, H)]
    peers = [(row + i) % R for i in range(1, R)]

    barrier = pltpu.get_barrier_semaphore()
    for c in hops + [mate]:
        pl.semaphore_signal(barrier, inc=1, device_id={"col": c}, device_id_type=MESH)
    for r in peers:
        pl.semaphore_signal(barrier, inc=1, device_id={"row": r}, device_id_type=MESH)

    @pl.when(z > 0)
    def _():
        pl.semaphore_signal(barrier, inc=1, device_id={"layer": z - 1}, device_id_type=MESH)

    @pl.when(z < L - 1)
    def _():
        pl.semaphore_signal(barrier, inc=1, device_id={"layer": z + 1}, device_id_type=MESH)

    tables = [sorted(range(L), key=lambda d: (-abs(d - i), -i if d > i else i - L + 1)) for i in range(L)]

    def pick(t):
        found = 0
        for i in range(L):
            found = found + jnp.where(z == i, tables[i][t], 0)
        return found

    dest = [pick(t) for t in range(L)]

    def load_panel(t):
        here = pl.ds(pl.multiple_of(dest[t] * rows, rows), rows)
        return pltpu.make_async_copy(panel_hbm.at[here], panel.at[here], lp.at[t])

    def load_slab(n):
        return pltpu.make_async_copy(
            slab_hbm.at[0, :, :, pl.ds(starts[n], widths[n])], slabs[n].at[pl.ds(row * mine, mine)], ls.at[n])

    small = [
        pltpu.make_async_copy(src, dst, lm.at[i])
        for i, (src, dst) in enumerate([(in_hbm, in_pat), (owner_hbm, owner), (out_hbm, out_pat)])
    ]
    small[0].start()
    load_panel(0).start()
    load_slab(0).start()
    for t in range(1, max(L, N)):
        if t < L:
            load_panel(t).start()
        if t < N:
            load_slab(t).start()
    small[1].start()
    small[2].start()

    def mask(t):
        for i in range(brows):
            first = pl.multiple_of(dest[t] * rows + i * bs, bs)
            for j in range(depth // bs):
                keep = in_pat[j, dest[t] * brows + i].astype(jnp.float32)
                block = panel[pl.ds(first, bs), j * bs : (j + 1) * bs].astype(jnp.float32)
                portion[col, t, i * bs : (i + 1) * bs, j * bs : (j + 1) * bs] = (block * keep).astype(jnp.bfloat16)

    def send_part(c_to, t, sem):
        return pltpu.make_async_remote_copy(
            src_ref=portion.at[col, t], dst_ref=portion.at[col, t], send_sem=sem, recv_sem=rp.at[col, t],
            device_id={"col": c_to}, device_id_type=MESH)

    def relay(c_from, t, sem):
        return pltpu.make_async_remote_copy(
            src_ref=portion.at[c_from, t], dst_ref=portion.at[c_from, t], send_sem=sem, recv_sem=rp.at[c_from, t],
            device_id={"col": mate}, device_id_type=MESH)

    def send_slab(r_to, i, n):
        block = slabs[n].at[pl.ds(row * mine, mine)]
        return pltpu.make_async_remote_copy(
            src_ref=block, dst_ref=block, send_sem=ss.at[i, n], recv_sem=rs.at[row, n],
            device_id={"row": r_to}, device_id_type=MESH)

    def start_parts(t):
        for i, c in enumerate(hops):
            send_part(c, t, sx.at[i, t]).start()
        send_part(mate, t, sc.at[t]).start()

    def start_slab(n):
        for i, r in enumerate(peers):
            send_slab(r, i, n).start()

    small[0].wait()
    load_panel(0).wait()
    mask(0)
    load_slab(0).wait()
    pl.semaphore_wait(barrier, (R - 1) + H + jnp.where(z > 0, 1, 0) + jnp.where(z < L - 1, 1, 0))
    start_slab(0)
    start_parts(0)
    for t in range(1, max(L, N)):
        if t < N:
            load_slab(t).wait()
            start_slab(t)
        if t < L:
            load_panel(t).wait()
            mask(t)
            start_parts(t)
    small[1].wait()
    small[2].wait()

    def ready_parts(t):
        for i, c in enumerate(hops):
            relay(c, t, sr.at[i, t]).wait_recv()
            relay(c, t, sr.at[i, t]).start()

    def wait_parts(t):
        for c in [mate] + relays:
            relay(c, t, sc.at[t]).wait_recv()

    def ready_slab(n):
        for r in peers:
            pltpu.make_async_remote_copy(
                src_ref=slabs[n].at[pl.ds(r * mine, mine)], dst_ref=slabs[n].at[pl.ds(r * mine, mine)],
                send_sem=ss.at[0, n], recv_sem=rs.at[r, n], device_id={"row": r}, device_id_type=MESH).wait_recv()
        for j in range(R * mine):
            ops[j * bs : (j + 1) * bs, starts[n] : starts[n] + widths[n]] = slabs[n][owner[0, j]]

    near = min(2, L - 1)

    def product(t, n):
        left = jnp.concatenate([portion[c, t] for c in range(C)], axis=1)
        return jnp.dot(left, ops[:, starts[n] : starts[n] + widths[n]], preferred_element_type=jnp.float32)

    def multiply_near():
        left = [portion[c, near:L].reshape((L - near) * rows, depth) for c in range(C)]
        acc[...] = jnp.dot(jnp.concatenate(left, axis=1), ops[...], preferred_element_type=jnp.float32)

    def message(t, n, slot, to):
        return pltpu.make_async_remote_copy(
            src_ref=sbufs[n].at[t], dst_ref=rbufs[n].at[slot], send_sem=sz.at[t, n], recv_sem=rz.at[slot, n],
            device_id={"layer": to}, device_id_type=MESH)

    def arrived(slot, n):
        message(0, n, slot, (z + 1) % L).wait_recv()
        return decode(rbufs[n].at[slot], rows)

    def route(t):
        up = jnp.where(dest[t] > z, 1, 0)
        return dest[t] + L * (1 - up), z + 2 * up - 1

    inner = (z > 0) & (z < L - 1)

    def pass_on(t, n, add):
        slot, to = route(t)
        if t < near:
            total = product(t, n)
        else:
            total = acc[(t - near) * rows : (t - near + 1) * rows, starts[n] : starts[n] + widths[n]]
        if add:
            total = total + arrived(slot, n)
        encode(total, sbufs[n].at[t])
        message(t, n, slot, to).start()

    def parts(*steps):
        for t in steps:
            ready_parts(t)
        for t in steps:
            wait_parts(t)

    def finish(n, up, down):
        here = slice(starts[n], starts[n] + widths[n])
        total = acc[(L - 1 - near) * rows :, here]
        if up:
            total = total + arrived(z, n)
        if down:
            total = total + arrived(z + L, n)
        for i in range(brows):
            for j in range(widths[n] // bs):
                keep = out_pat[i, starts[n] // bs + j].astype(jnp.float32)
                block = total[i * bs : (i + 1) * bs, j * bs : (j + 1) * bs] * keep
                first = starts[n] + j * bs
                out[i * bs : (i + 1) * bs, first : first + bs] = block.astype(jnp.bfloat16)

    late = list(range(near, L))
    tail = [(t, n) for t in range(2, L - 1) for n in range(N)]

    @pl.when(jnp.logical_not(inner))
    def _():
        for n in range(N):
            if n == 0:
                ready_parts(0)
            ready_slab(n)
            if n == 0:
                wait_parts(0)
            pass_on(0, n, False)
            if n == 1 and near > 1:
                parts(1)
                pass_on(1, 0, False)
            if n > 0 and near > 1:
                pass_on(1, n, False)
        parts(*late)
        multiply_near()
        for t, n in tail:
            pass_on(t, n, False)

        @pl.when(z > 0)
        def _():
            for n in range(N):
                finish(n, True, False)

        @pl.when(z == 0)
        def _():
            for n in range(N):
                finish(n, False, L > 1)

    if L > 2:

        @pl.when(inner)
        def _():
            for n in range(N):
                if n == 0:
                    ready_parts(0)
                ready_slab(n)
                if n == 0:
                    wait_parts(0)
                if n == N - 1:
                    parts(*late)
                    multiply_near()
                    if N > 2:
                        pass_on(1, N - 3, True)
                pass_on(0, n, True)
                if n == 0:
                    parts(1)
                elif n < N - 1 and n > 1:
                    pass_on(1, n - 2, True)
            order = [(1, n) for n in range(max(N - 2, 0), N)]
            for t, n in order + tail:
                pass_on(t, n, True)
            for n in range(N):
                finish(n, True, True)

    for t in range(L):
        for i, c in enumerate(hops):
            send_part(c, t, sx.at[i, t]).wait_send()
            relay(c, t, sr.at[i, t]).wait_send()
        send_part(mate, t, sc.at[t]).wait_send()
    for n in range(N):
        for i, r in enumerate(peers):
            send_slab(r, i, n).wait_send()
        for t in range(L - 1):
            slot, to = route(t)
            message(t, n, slot, to).wait_send()


def solution(mesh):
    R, C, L = (mesh.shape[name] for name in ("row", "col", "layer"))

    def shards(panel, in_pat, slab, owner, out_pat):
        bs, cols = slab.shape[2], slab.shape[3]
        rows = panel.shape[0] // L
        depth = panel.shape[2]
        blocks = R * slab.shape[1]
        widths = (cols // 4,) * 4
        N = len(widths)
        H = C // 2
        dma = pltpu.SemaphoreType.DMA
        vmem = pl.BlockSpec(memory_space=pltpu.VMEM)
        hbm = pl.BlockSpec(memory_space=pltpu.HBM)
        return pl.pallas_call(
            functools.partial(kernel, (R, C, L), widths),
            out_shape=jax.ShapeDtypeStruct((rows, cols), jnp.bfloat16),
            in_specs=[hbm] * 5,
            out_specs=vmem,
            scratch_shapes=[pltpu.VMEM((blocks, bs, w), jnp.bfloat16) for w in widths]
            + [pltpu.VMEM((L - 1, rows + PAD, w), jnp.int16) for w in widths]
            + [pltpu.VMEM((2 * L, rows + PAD, w), jnp.int16) for w in widths]
            + [
                pltpu.VMEM((blocks * bs, cols), jnp.bfloat16),
                pltpu.VMEM((panel.shape[0], depth), jnp.bfloat16),
                pltpu.SMEM((in_pat.shape[2], in_pat.shape[0]), jnp.int32),
                pltpu.SMEM(owner.shape, jnp.int32),
                pltpu.SMEM(out_pat.shape, jnp.int32),
                pltpu.VMEM((C, L, rows, depth), jnp.bfloat16),
                pltpu.VMEM(((L - min(2, L - 1)) * rows, cols), jnp.float32),
                dma((L,)),
                dma((N,)),
                dma((3,)),
                dma((H - 1, L)),
                dma((L,)),
                dma((H - 1, L)),
                dma((C, L)),
                dma((R - 1, N)),
                dma((R, N)),
                dma((L - 1, N)),
                dma((2 * L, N)),
            ],
            compiler_params=pltpu.CompilerParams(
                collective_id=0, has_side_effects=True, vmem_limit_bytes=int(53.4 * 2**20)),
        )(panel.reshape(panel.shape[0], depth), in_pat[:, 0, :].T, slab, owner, out_pat)

    in_specs = (
        P("row", "layer", "col"),
        P("row", "layer", "col"),
        P("layer", "row", None, "col"),
        P("layer", None),
        P(("row", "layer"), "col"),
    )
    out_specs = P(("row", "layer"), "col")
    return jax.shard_map(shards, mesh=mesh, in_specs=in_specs, out_specs=out_specs, check_vma=False)
```

```python
import functools

import jax
import jax.numpy as jnp
from jax import lax
from jax.experimental import pallas as pl
from jax.experimental.pallas import tpu as pltpu
from jax.sharding import PartitionSpec as P

MESH = pl.DeviceIdType.MESH
STEPS = 128.0
TOP = 32640.0
PAD = 16


def encode(values, out):
    rows = values.shape[0]
    peak = jnp.maximum(jnp.max(jnp.abs(values), axis=0, keepdims=True), 2.0**-100)
    level = jnp.ceil(jnp.log2(peak) * STEPS + 0.5)
    factor = jnp.exp2(level * (-1.0 / STEPS)) * TOP
    coded = jnp.round(values * factor).astype(jnp.int32)
    out[0:rows, :] = coded.astype(jnp.int16)
    wide = jnp.broadcast_to(level, (PAD, values.shape[1]))
    out[rows : rows + PAD, :] = wide.astype(jnp.int32).astype(jnp.int16)


def decode(message, rows):
    level = message[rows : rows + PAD, :].astype(jnp.int32).astype(jnp.float32)[0:1, :]
    factor = jnp.exp2(level * (1.0 / STEPS)) * (1.0 / TOP)
    return message[0:rows, :].astype(jnp.int32).astype(jnp.float32) * factor


def kernel(sizes, widths, panel_hbm, in_hbm, slab_hbm, owner_hbm, out_hbm, out, *scratch):
    R, C, L = sizes
    N = len(widths)
    starts = [sum(widths[:n]) for n in range(N)]
    slabs, sbufs, rbufs = (scratch[i * N : (i + 1) * N] for i in range(3))
    ops, panel, in_pat, owner, out_pat, portion, acc, lp, ls, lm, sx, sc, sr, rp, ss, rs, sz, rz = scratch[3 * N :]
    H = C // 2
    row, col, z = lax.axis_index("row"), lax.axis_index("col"), lax.axis_index("layer")
    half, side = col // 2, col % 2
    mate = half * 2 + (1 - side)
    rows = out.shape[0]
    bs = slab_hbm.shape[2]
    depth = panel.shape[1]
    mine = slab_hbm.shape[1]
    brows = rows // bs
    hops = [((half + i) % H) * 2 + side for i in range(1, H)]
    relays = [((half + i) % H) * 2 + (1 - side) for i in range(1, H)]
    peers = [(row + i) % R for i in range(1, R)]

    barrier = pltpu.get_barrier_semaphore()
    for c in hops + [mate]:
        pl.semaphore_signal(barrier, inc=1, device_id={"col": c}, device_id_type=MESH)
    for r in peers:
        pl.semaphore_signal(barrier, inc=1, device_id={"row": r}, device_id_type=MESH)

    @pl.when(z > 0)
    def _():
        pl.semaphore_signal(barrier, inc=1, device_id={"layer": z - 1}, device_id_type=MESH)

    @pl.when(z < L - 1)
    def _():
        pl.semaphore_signal(barrier, inc=1, device_id={"layer": z + 1}, device_id_type=MESH)

    tables = [sorted(range(L), key=lambda d: (-abs(d - i), -i if d > i else i - L + 1)) for i in range(L)]

    def pick(t):
        found = 0
        for i in range(L):
            found = found + jnp.where(z == i, tables[i][t], 0)
        return found

    dest = [pick(t) for t in range(L)]

    def load_panel(t):
        here = pl.ds(pl.multiple_of(dest[t] * rows, rows), rows)
        return pltpu.make_async_copy(panel_hbm.at[here], panel.at[here], lp.at[t])

    def load_slab(n):
        return pltpu.make_async_copy(
            slab_hbm.at[0, :, :, pl.ds(starts[n], widths[n])], slabs[n].at[pl.ds(row * mine, mine)], ls.at[n])

    small = [
        pltpu.make_async_copy(src, dst, lm.at[i])
        for i, (src, dst) in enumerate([(in_hbm, in_pat), (owner_hbm, owner), (out_hbm, out_pat)])
    ]
    small[0].start()
    load_panel(0).start()
    load_slab(0).start()
    for t in range(1, max(L, N)):
        if t < L:
            load_panel(t).start()
        if t < N:
            load_slab(t).start()
    small[1].start()
    small[2].start()

    def mask(t):
        for i in range(brows):
            first = pl.multiple_of(dest[t] * rows + i * bs, bs)
            for j in range(depth // bs):
                keep = in_pat[j, dest[t] * brows + i].astype(jnp.float32)
                block = panel[pl.ds(first, bs), j * bs : (j + 1) * bs].astype(jnp.float32)
                portion[col, t, i * bs : (i + 1) * bs, j * bs : (j + 1) * bs] = (block * keep).astype(jnp.bfloat16)

    def send_part(c_to, t, sem):
        return pltpu.make_async_remote_copy(
            src_ref=portion.at[col, t], dst_ref=portion.at[col, t], send_sem=sem, recv_sem=rp.at[col, t],
            device_id={"col": c_to}, device_id_type=MESH)

    def relay(c_from, t, sem):
        return pltpu.make_async_remote_copy(
            src_ref=portion.at[c_from, t], dst_ref=portion.at[c_from, t], send_sem=sem, recv_sem=rp.at[c_from, t],
            device_id={"col": mate}, device_id_type=MESH)

    def send_slab(r_to, i, n):
        block = slabs[n].at[pl.ds(row * mine, mine)]
        return pltpu.make_async_remote_copy(
            src_ref=block, dst_ref=block, send_sem=ss.at[i, n], recv_sem=rs.at[row, n],
            device_id={"row": r_to}, device_id_type=MESH)

    def start_parts(t):
        for i, c in enumerate(hops):
            send_part(c, t, sx.at[i, t]).start()
        send_part(mate, t, sc.at[t]).start()

    def start_slab(n):
        for i, r in enumerate(peers):
            send_slab(r, i, n).start()

    small[0].wait()
    load_panel(0).wait()
    mask(0)
    load_slab(0).wait()
    pl.semaphore_wait(barrier, (R - 1) + H + jnp.where(z > 0, 1, 0) + jnp.where(z < L - 1, 1, 0))
    start_slab(0)
    start_parts(0)
    for t in range(1, max(L, N)):
        if t < N:
            load_slab(t).wait()
            start_slab(t)
        if t < L:
            load_panel(t).wait()
            mask(t)
            start_parts(t)
    small[1].wait()
    small[2].wait()

    def ready_parts(t):
        for i, c in enumerate(hops):
            relay(c, t, sr.at[i, t]).wait_recv()
            relay(c, t, sr.at[i, t]).start()

    def wait_parts(t):
        for c in [mate] + relays:
            relay(c, t, sc.at[t]).wait_recv()

    def ready_slab(n):
        for r in peers:
            pltpu.make_async_remote_copy(
                src_ref=slabs[n].at[pl.ds(r * mine, mine)], dst_ref=slabs[n].at[pl.ds(r * mine, mine)],
                send_sem=ss.at[0, n], recv_sem=rs.at[r, n], device_id={"row": r}, device_id_type=MESH).wait_recv()
        for j in range(R * mine):
            ops[j * bs : (j + 1) * bs, starts[n] : starts[n] + widths[n]] = slabs[n][owner[0, j]]

    near = min(2, L - 1)

    def product(t, n):
        left = jnp.concatenate([portion[c, t] for c in range(C)], axis=1)
        return jnp.dot(left, ops[:, starts[n] : starts[n] + widths[n]], preferred_element_type=jnp.float32)

    def multiply_near():
        left = [portion[c, near:L].reshape((L - near) * rows, depth) for c in range(C)]
        acc[...] = jnp.dot(jnp.concatenate(left, axis=1), ops[...], preferred_element_type=jnp.float32)

    def message(t, n, slot, to):
        return pltpu.make_async_remote_copy(
            src_ref=sbufs[n].at[t], dst_ref=rbufs[n].at[slot], send_sem=sz.at[t, n], recv_sem=rz.at[slot, n],
            device_id={"layer": to}, device_id_type=MESH)

    def arrived(slot, n):
        message(0, n, slot, (z + 1) % L).wait_recv()
        return decode(rbufs[n].at[slot], rows)

    def route(t):
        up = jnp.where(dest[t] > z, 1, 0)
        return dest[t] + L * (1 - up), z + 2 * up - 1

    inner = (z > 0) & (z < L - 1)

    def pass_on(t, n, add):
        slot, to = route(t)
        if t < near:
            total = product(t, n)
        else:
            total = acc[(t - near) * rows : (t - near + 1) * rows, starts[n] : starts[n] + widths[n]]
        if add:
            total = total + arrived(slot, n)
        encode(total, sbufs[n].at[t])
        message(t, n, slot, to).start()

    def parts(*steps):
        for t in steps:
            ready_parts(t)
        for t in steps:
            wait_parts(t)

    def finish(n, up, down):
        here = slice(starts[n], starts[n] + widths[n])
        total = acc[(L - 1 - near) * rows :, here]
        if up:
            total = total + arrived(z, n)
        if down:
            total = total + arrived(z + L, n)
        for i in range(brows):
            for j in range(widths[n] // bs):
                keep = out_pat[i, starts[n] // bs + j].astype(jnp.float32)
                block = total[i * bs : (i + 1) * bs, j * bs : (j + 1) * bs] * keep
                first = starts[n] + j * bs
                out[i * bs : (i + 1) * bs, first : first + bs] = block.astype(jnp.bfloat16)

    late = list(range(near, L))
    tail = [(t, n) for t in range(2, L - 1) for n in range(N)]

    @pl.when(jnp.logical_not(inner))
    def _():
        for n in range(N):
            if n == 0:
                ready_parts(0)
            ready_slab(n)
            if n == 0:
                wait_parts(0)
            pass_on(0, n, False)
            if n == 1 and near > 1:
                parts(1)
                pass_on(1, 0, False)
            if n > 0 and near > 1:
                pass_on(1, n, False)
        parts(*late)
        multiply_near()
        for t, n in tail:
            pass_on(t, n, False)

        @pl.when(z > 0)
        def _():
            for n in range(N):
                finish(n, True, False)

        @pl.when(z == 0)
        def _():
            for n in range(N):
                finish(n, False, L > 1)

    if L > 2:

        @pl.when(inner)
        def _():
            for n in range(N):
                if n == 0:
                    ready_parts(0)
                ready_slab(n)
                if n == 0:
                    wait_parts(0)
                if n == N - 1:
                    parts(*late)
                    multiply_near()
                    if N > 2:
                        pass_on(1, N - 3, True)
                pass_on(0, n, True)
                if n == 0:
                    parts(1)
                elif n < N - 1 and n > 1:
                    pass_on(1, n - 2, True)
            order = [(1, n) for n in range(max(N - 2, 0), N)]
            for i, (t, n) in enumerate(tail):
                if i < len(order):
                    pass_on(*order[i], True)
                pass_on(t, n, True)
            for t, n in order[len(tail) :]:
                pass_on(t, n, True)
            for n in range(N):
                finish(n, True, True)

    for t in range(L):
        for i, c in enumerate(hops):
            send_part(c, t, sx.at[i, t]).wait_send()
            relay(c, t, sr.at[i, t]).wait_send()
        send_part(mate, t, sc.at[t]).wait_send()
    for n in range(N):
        for i, r in enumerate(peers):
            send_slab(r, i, n).wait_send()
        for t in range(L - 1):
            slot, to = route(t)
            message(t, n, slot, to).wait_send()


def solution(mesh):
    R, C, L = (mesh.shape[name] for name in ("row", "col", "layer"))

    def shards(panel, in_pat, slab, owner, out_pat):
        bs, cols = slab.shape[2], slab.shape[3]
        rows = panel.shape[0] // L
        depth = panel.shape[2]
        blocks = R * slab.shape[1]
        widths = (cols // 4,) * 4
        N = len(widths)
        H = C // 2
        dma = pltpu.SemaphoreType.DMA
        vmem = pl.BlockSpec(memory_space=pltpu.VMEM)
        hbm = pl.BlockSpec(memory_space=pltpu.HBM)
        return pl.pallas_call(
            functools.partial(kernel, (R, C, L), widths),
            out_shape=jax.ShapeDtypeStruct((rows, cols), jnp.bfloat16),
            in_specs=[hbm] * 5,
            out_specs=vmem,
            scratch_shapes=[pltpu.VMEM((blocks, bs, w), jnp.bfloat16) for w in widths]
            + [pltpu.VMEM((L - 1, rows + PAD, w), jnp.int16) for w in widths]
            + [pltpu.VMEM((2 * L, rows + PAD, w), jnp.int16) for w in widths]
            + [
                pltpu.VMEM((blocks * bs, cols), jnp.bfloat16),
                pltpu.VMEM((panel.shape[0], depth), jnp.bfloat16),
                pltpu.SMEM((in_pat.shape[2], in_pat.shape[0]), jnp.int32),
                pltpu.SMEM(owner.shape, jnp.int32),
                pltpu.SMEM(out_pat.shape, jnp.int32),
                pltpu.VMEM((C, L, rows, depth), jnp.bfloat16),
                pltpu.VMEM(((L - min(2, L - 1)) * rows, cols), jnp.float32),
                dma((L,)),
                dma((N,)),
                dma((3,)),
                dma((H - 1, L)),
                dma((L,)),
                dma((H - 1, L)),
                dma((C, L)),
                dma((R - 1, N)),
                dma((R, N)),
                dma((L - 1, N)),
                dma((2 * L, N)),
            ],
            compiler_params=pltpu.CompilerParams(
                collective_id=0, has_side_effects=True, vmem_limit_bytes=int(53.4 * 2**20)),
        )(panel.reshape(panel.shape[0], depth), in_pat[:, 0, :].T, slab, owner, out_pat)

    in_specs = (
        P("row", "layer", "col"),
        P("row", "layer", "col"),
        P("layer", "row", None, "col"),
        P("layer", None),
        P(("row", "layer"), "col"),
    )
    out_specs = P(("row", "layer"), "col")
    return jax.shard_map(shards, mesh=mesh, in_specs=in_specs, out_specs=out_specs, check_vma=False)
```
